1024 devices in a mesh: shot: 32 (over y, x_hi, core), slab: 32 (over z, x_lo).
Axes of the slice: x: 4 (x_hi: 2, x_lo: 2; x = x_hi * 2 + x_lo), y: 8, z: 16, core: 2. Of those that a mesh axis runs over, the one named last changes fastest.
Arguments:
- courant: float32 [128, 32, 128], P('slab'), may hold values from 0.04 to 0.16
- buoyancy: float32 [128, 32, 128], P('slab'), may hold values from 0.5 to 2
- wave_before: float32 [32, 128, 32, 128], P('shot', 'slab'), may hold values from -6 to 6
- wave_now: float32 [32, 128, 32, 128], P('shot', 'slab'), may hold values from -6 to 6
- wavelet: float32 [32, 6], P('shot'), may hold values from -16 to 16
- source_cell: int32 [32, 1], P('shot'), may hold values from 0 to 524287
- observed: float32 [32, 6, 16384], P('shot', None, 'slab'), may hold values from -6 to 6
- receiver_slab: int32 [32, 16384, 1], P('shot', 'slab'), may hold values from 0 to 31; in each aligned block of 512 rows (0 to 511, 512 to 1023, ..., all dimensions but the last counted through in order) at most 32 rows name the same one
- receiver_cell: int32 [32, 16384], P('shot', 'slab'), may hold values from 0 to 16383
Outputs:
- grad_courant: float32 [128, 32, 128], P('slab')
- grad_buoyancy: float32 [128, 32, 128], P('slab')
The draws below stay inside these ranges and needn't reach their ends.
Inputs may be any that keep to these rules, and one draw needn't show every extreme that they name: `receiver_slab`: among the receivers held by one device no slab is named more than 32 times; for some devices one slab is named exactly 32 times.
All inputs are finite; a program needn't handle non-finite values.
Results may differ from the reference program's by a relative error of at most 0.0003.
Values sent between devices are 32-bit elements; how exact they have to be, the bound alone decides.
No kernel may reach another device: no remote copies, remote signals or barrier semaphores. Data moves between devices by JAX's collectives and lax.ppermute only.
A program may use at most 32 MiB of HBM per device.

```python
import math
import jax
import jax.numpy as jnp
import numpy as np
from jax import lax

CX = 4
NZ = 32
NY = 128
REC_DEV = 512
STEPS = 6
NX = 128
SHOTS = 32
REC = 16384
CAP = 32
N_SLAB = 32


def place_ends(array, own_key, least, top_value):
    longest = array.shape.index(max(array.shape))
    spots = []
    for shift in (0, 1):
        where = [jax.random.randint(jax.random.fold_in(own_key, axis), (), 0, length) for axis, length in enumerate(array.shape)]
        where[longest] = (where[longest] + shift) % array.shape[longest]
        spots.append(tuple(where))
    return array.at[spots[0]].set(least).at[spots[1]].set(top_value)


def levels(stream_key, shape, split, low, top_value):
    gain, own = 1.0, jax.random.fold_in(stream_key, 6)
    for dim, blocks in split:
        steps = jnp.exp(jax.random.uniform(jax.random.fold_in(own, dim), (blocks,), jnp.float32, low / len(split), top_value / len(split)))
        gain = gain * jnp.repeat(steps, shape[dim] // blocks).reshape([-1 if axis == dim else 1 for axis in range(len(shape))])
    return gain


def routed_block(own_key, own, number, rows, count, top, bound, lean):
    ranking = jax.random.permutation(own_key, count)
    packed, ordinary = portions_of(count, rows * top, bound, lean, True), portions_of(count, rows * top, bound, lean, False)
    places = jnp.arange(count)

    def named(tallies, turn):
        used = int((tallies > 0).sum())
        fixed = max(1, used // 4)
        shifted = fixed + (places - fixed + turn * (used - fixed)) % max(1, count - fixed)
        return jnp.zeros((count,), jnp.int32).at[ranking[jnp.where(places < fixed, places, shifted)]].set(jnp.asarray(tallies, jnp.int32))

    tallies = jnp.where(number % 4 == 0, named(packed, number // 4), named(ordinary, number - number // 4 - 1))
    mixed = jax.random.permutation(jax.random.fold_in(own, 3), count)
    source_of, taker = mixed[0:count // 2 * 2:2], mixed[1:count // 2 * 2:2]
    margin = jnp.minimum(tallies[source_of] - 1, bound - tallies[taker]) // 2
    margin = jnp.where((source_of == ranking[0]) | (taker == ranking[0]) | (tallies[taker] == 0), 0, jnp.maximum(margin, 0))
    shifted = jax.random.randint(jax.random.fold_in(own, 4), (count // 2,), 0, 1 << 20) % (margin + 1)
    tallies = tallies.at[source_of].add(-shifted).at[taker].add(shifted)
    labels = jnp.searchsorted(jnp.cumsum(tallies), jnp.arange(rows * top), side="right").astype(jnp.int32)
    grid = labels.reshape(top, rows).T
    grid = grid[jax.random.permutation(jax.random.fold_in(own, 1), rows)]
    turn = jax.random.randint(jax.random.fold_in(own, 2), (rows, 1), 0, top)
    return jnp.take_along_axis(grid, (jnp.arange(top)[None, :] + turn) % top, axis=1)


def portions_of(amount, total, limit, slope, full):
    weights = [(1 << 20) // math.isqrt(rank ** slope) + 1 for rank in range(1, amount + 1)]
    largest = limit if full else min(limit, max(-(-total // amount), total * weights[0] // sum(weights)))
    least = 1 if total - largest >= amount - 1 else 0
    given, spare = [largest] + [least] * (amount - 1), total - largest - least * (amount - 1)
    while spare > 0:
        free = [i for i in range(1, amount) if given[i] < largest] or [i for i in range(1, amount) if given[i] < limit]
        whole, budget = sum([weights[i] for i in free]), spare
        for i in free:
            more = min(limit - given[i], max(1, budget * weights[i] // whole), spare)
            given[i] = given[i] + more
            spare = spare - more
    return np.array(given)


def centred(stream_key, dims, spread, limit, pieces=(), kind=jnp.bfloat16):
    array = spread * jax.random.normal(stream_key, dims, jnp.float32)
    if pieces:
        array = array * levels(stream_key, dims, pieces, -0.22, 0.18)
    return jnp.clip(array, -limit, limit).astype(kind)


def setup_inputs(seed: int = 0) -> dict:
    keys = jax.random.split(jax.random.key(seed), 10)
    courant = jnp.clip(0.04 + 0.12 * jax.random.uniform(keys[0], (NX, NZ, NY), jnp.float32) ** levels(keys[0], (NX, NZ, NY), ((0, 32),), -0.2, 0.2), 0.04, 0.16)
    buoyancy = jnp.clip(jnp.exp(math.log(2.0) - 1.3862944 * jax.random.uniform(keys[1], (NX, NZ, NY), jnp.float32) ** levels(keys[1], (NX, NZ, NY), ((0, 32),), -0.2, 0.2)), 0.5, 2.0)
    wave_before = centred(keys[2], (SHOTS, NX, NZ, NY), 1.0, 6.0, ((0, 32), (1, 32)), jnp.float32)
    wave_now = centred(keys[3], (SHOTS, NX, NZ, NY), 1.0, 6.0, ((0, 32), (1, 32)), jnp.float32)
    wavelet = centred(keys[4], (SHOTS, STEPS), 3.0, 16.0, ((0, 32),), jnp.float32)
    source_cell = place_ends(jax.random.randint(keys[5], (SHOTS, 1), 0, NX * NZ * NY), jax.random.fold_in(keys[5], 1), 0, (NX * NZ * NY) - 1).astype(jnp.int32)
    observed = centred(keys[6], (SHOTS, STEPS, REC), 1.0, 6.0, ((0, 32), (2, 32)), jnp.float32)
    receiver_slab_keys = jax.random.split(jax.random.fold_in(keys[7], 1), SHOTS * REC // REC_DEV)
    receiver_slab_turns = jax.random.permutation(jax.random.fold_in(keys[7], 3), SHOTS * REC // REC_DEV)
    receiver_slab = jax.vmap(lambda own, number: routed_block(jax.random.fold_in(keys[7], 2), own, number, REC_DEV, N_SLAB, 1, CAP, 2))(receiver_slab_keys, receiver_slab_turns).reshape((SHOTS, REC, 1))
    receiver_cell = place_ends(jax.random.randint(keys[8], (SHOTS, REC), 0, CX * NZ * NY), jax.random.fold_in(keys[8], 1), 0, (CX * NZ * NY) - 1).astype(jnp.int32)
    return dict(courant=courant, buoyancy=buoyancy, wave_before=wave_before, wave_now=wave_now, wavelet=wavelet, source_cell=source_cell, observed=observed, receiver_slab=receiver_slab, receiver_cell=receiver_cell)


def neighbours(padded):
    return [padded[2:, 1:-1, 1:-1], padded[:-2, 1:-1, 1:-1], padded[1:-1, 2:, 1:-1], padded[1:-1, :-2, 1:-1], padded[1:-1, 1:-1, 2:], padded[1:-1, 1:-1, :-2]]

def operate_padded(padded_wave, padded_buoy):
    centre = padded_wave[1:-1, 1:-1, 1:-1]
    buoy_centre = padded_buoy[1:-1, 1:-1, 1:-1]
    summed = jnp.zeros_like(centre)
    for wave_side, buoy_side in zip(neighbours(padded_wave), neighbours(padded_buoy)):
        summed = summed + 0.5 * (buoy_centre + buoy_side) * (wave_side - centre)
    return summed

def shot_loss(courant, buoyancy, wave_before, wave_now, pulses, source, traces, rec_slab, rec_cell):
    grid_shape = courant.shape
    glob_index = (rec_slab * (CX * NZ * NY) + rec_cell).astype(jnp.int32)
    padded_buoy = jnp.pad(buoyancy, 1)
    misfit = jnp.zeros((), courant.dtype)
    for n in range(STEPS):
        laplace = operate_padded(jnp.pad(wave_now, 1), padded_buoy)
        next_wave = 2.0 * wave_now - wave_before + courant * laplace
        next_wave = next_wave.reshape(-1).at[source].add(pulses[n]).reshape(grid_shape)
        predicted = next_wave.reshape(-1)[glob_index]
        residual = predicted - traces[n]
        misfit = misfit + 0.5 * jnp.sum(residual * residual)
        wave_before, wave_now = (wave_now, next_wave)
    return misfit

def reference(courant, buoyancy, wave_before, wave_now, wavelet, source_cell, observed, receiver_slab, receiver_cell):
    gradient = jax.grad(shot_loss, argnums=(0, 1))

    def one_shot(carry, shot):
        before, present_wave, pulses, source, traces, slabs, cells = shot
        grad_q, grad_b = gradient(courant, buoyancy, before, present_wave, pulses, source, traces, slabs, cells)
        return ((carry[0] + grad_q, carry[1] + grad_b), None)
    zeros = jnp.zeros_like(courant)
    totals, unused = lax.scan(one_shot, (zeros, zeros), (wave_before, wave_now, wavelet, source_cell[:, 0], observed, receiver_slab[:, :, 0], receiver_cell))
    return (totals[0], totals[1])
```

```python
import jax
import jax.numpy as jnp
from jax import lax
from jax.experimental import pallas as pl
from jax.experimental.pallas import tpu as pltpu
from jax.sharding import PartitionSpec as P

STEPS = 6
NZ = 32
NY = 128
ROWS = 4
PLANE = NZ * NY
SLABS = 32
SHOTS = 32
CAP = 32
REACH = 3
EXT = ROWS * (2 * REACH + 1)
OWN = ROWS * REACH
LO = 4
BAND = 20

NT = (((1,), (1,)), ((), ()))


def split_bf16(x, pieces):
    out = []
    for _ in range(pieces):
        part = x.astype(jnp.bfloat16)
        out.append(part)
        x = x - part.astype(jnp.float32)
    return out


def iota(shape, axis):
    return lax.broadcasted_iota(jnp.int32, shape, axis)


def mxu(a, b, dims):
    return lax.dot_general(a, b, dims, preferred_element_type=jnp.float32)


def route_kernel(slab_ref, cell_ref, obs_ref, out_ref):
    rec = slab_ref.shape[1]
    slab = slab_ref[...]
    hot = (iota((SLABS, rec), 0) == slab).astype(jnp.float32)
    hot16 = hot.astype(jnp.bfloat16)
    tri = (iota((rec, rec), 0) < iota((rec, rec), 1)).astype(jnp.float32).astype(jnp.bfloat16)
    earlier = mxu(hot16, tri, (((1,), (0,)), ((), ())))
    rank = jnp.sum(earlier * hot, axis=0, keepdims=True).astype(jnp.int32)
    at_slot = iota((CAP, rec), 0) == rank
    cells = (cell_ref[...] + 1).astype(jnp.float32)
    values = [obs_ref[n : n + 1, :] for n in range(STEPS)] + [cells]
    total = None
    splits = [split_bf16(v, 3) for v in values]
    for p in range(3):
        rows = [jnp.where(at_slot, s[p].astype(jnp.float32), 0.0) for s in splits]
        rows.append(jnp.zeros((CAP, rec), jnp.float32))
        block = jnp.concatenate(rows, axis=0).astype(jnp.bfloat16)
        term = mxu(hot16, block, NT)
        total = term if total is None else total + term
    row = iota((SLABS, 128), 0)
    lane = iota((SLABS, 128), 1)

    def shifted(tile, shift):
        moved = pltpu.roll(tile, (-shift) % SLABS, 0)
        there = row + shift
        return jnp.where((there >= 0) & (there < SLABS), moved, 0.0)

    tiles = [total[:, 128 * t : 128 * t + 128] for t in range(2)]
    by_shift = {s: [shifted(t, s) if s else t for t in tiles] for s in (-2, -1, 0, 1, 2)}

    def piece(shift, value, group):
        tile = by_shift[shift][value // 4]
        return pltpu.roll(tile, (CAP * (group - value % 4)) % 128, 1) if (group - value % 4) % 4 else tile

    for v in range(8):
        if v < 7:
            near = jnp.where(lane < CAP, piece(-1, v, 0), jnp.where(lane < 2 * CAP, piece(0, v, 1), piece(1, v, 2)))
        else:
            near = jnp.zeros((SLABS, 128), jnp.float32)
        if v < 3:
            far = piece(-2, v + 4, 3)
        elif v < 6:
            far = piece(2, v + 1, 3)
        else:
            far = jnp.zeros((SLABS, 128), jnp.float32)
        out_ref[:, v, :] = jnp.where(lane < 3 * CAP, near, far)


def scatter_dense(cell_row, value_rows, halves):
    count = cell_row.shape[1]
    cell = cell_row.astype(jnp.int32) - 1
    half = lax.shift_right_arithmetic(cell, 13)
    lane_of = cell & 127
    if halves is None:
        spot, width = half * 128 + lane_of, 256
    else:
        spot, width = jnp.where(half == halves, lane_of, -1), 128
    right = (iota((width, count), 0) == spot).astype(jnp.float32).astype(jnp.bfloat16)
    left_hot = iota((64, count), 0) == (lax.shift_right_arithmetic(cell, 7) & 63)
    zero = jnp.zeros((64, count), jnp.float32)
    splits = [split_bf16(v, 2) for v in value_rows]
    blocks = [jnp.where(left_hot, 1.0, zero).astype(jnp.bfloat16)]
    lows = []
    for s in splits:
        blocks.append(jnp.where(left_hot, s[0].astype(jnp.float32), zero).astype(jnp.bfloat16))
        lows.append(jnp.where(left_hot, s[1].astype(jnp.float32), zero).astype(jnp.bfloat16))
    main = mxu(jnp.concatenate(blocks, axis=0), right, NT)
    rest = mxu(jnp.concatenate(lows, axis=0), right, NT)
    out = [main[0:64]]
    for i in range(len(splits)):
        out.append(main[64 * (i + 1) : 64 * (i + 2)] + rest[64 * i : 64 * (i + 1)])
    return out


def window_kernel(
    source_ref,
    pulse_ref,
    mine_ref,
    *refs,
):
    near_refs = refs[: 2 * REACH]
    got_ref = refs[2 * REACH]
    out_ref = refs[2 * REACH + 1]
    (
        ext,
        wave,
        cx,
        cy,
        cz,
        edge,
        lap,
        count,
        traces,
        adj,
        weighted,
    ) = refs[2 * REACH + 2 :]
    slab = lax.axis_index("slab")

    for f in range(2):
        ext[f, OWN : OWN + ROWS] = mine_ref[f]
    for f in (2, 3):
        wave[f - 2, OWN : OWN + ROWS] = mine_ref[f]
    for i, ref in enumerate(near_refs):
        distance, odd = i // 2 + 1, i % 2
        parity = lax.rem(lax.div(slab, distance), 2)
        side = jnp.where(parity == odd, distance, -distance)
        start = OWN + ROWS * side
        for f in range(2):
            ext[f, pl.ds(start, ROWS)] = ref[f]
            wave[f, pl.ds(start, ROWS)] = ref[f + 2]

    zpos = iota((NZ, NY), 0)
    ypos = iota((NZ, NY), 1)
    z_last, y_last = zpos == NZ - 1, ypos == NY - 1
    z_first, y_first = zpos == 0, ypos == 0

    def up_z(x):
        return pltpu.roll(x, NZ - 1, 0)

    def down_z(x):
        return pltpu.roll(x, 1, 0)

    def up_y(x):
        return pltpu.roll(x, NY - 1, 1)

    def down_y(x):
        return pltpu.roll(x, 1, 1)

    half_edge = 0.5 * ((z_first | z_last).astype(jnp.float32) + (y_first | y_last).astype(jnp.float32))
    for r in range(EXT):
        b = ext[1, r]
        if r + 1 < EXT:
            cx[r] = 0.5 * (b + ext[1, r + 1])
        cz[r] = jnp.where(z_last, 0.0, 0.5 * (b + up_z(b)))
        cy[r] = jnp.where(y_last, 0.0, 0.5 * (b + up_y(b)))
        edge[r] = half_edge * b

    def operate(load, lo, hi, emit):
        here = load(lo)
        below = cx[lo - 1] * (here - load(lo - 1))
        for r in range(lo, hi):
            above_row = load(r + 1)
            above = cx[r] * (above_row - here)
            flux_z = cz[r] * (up_z(here) - here)
            flux_y = cy[r] * (up_y(here) - here)
            total = (above - below) + (flux_z - down_z(flux_z)) + (flux_y - down_y(flux_y)) - edge[r] * here
            emit(r, here, total)
            here, below = above_row, above

    local_source = source_ref[0, 0] - (slab * ROWS - OWN) * PLANE
    flat = zpos * NY + ypos

    for n in range(STEPS):
        reach = OWN - 1 - n
        pulse = pulse_ref[0, n]

        def emit(r, here, total, n=n, pulse=pulse):
            if OWN <= r < OWN + ROWS:
                lap[n, r - OWN] = total
            fresh = 2.0 * here - wave[n, r] + ext[0, r] * total
            wave[n + 2, r] = fresh + jnp.where(flat == local_source - r * PLANE, pulse, 0.0)

        operate(lambda r, n=n: wave[n + 1, r], OWN - reach, OWN + ROWS + reach, emit)

    lane8 = iota((8, 128), 1)
    blocks = [[], [], [], []]
    for j in range(SLABS // 4):
        quad = [got_ref[4 * j + i] for i in range(4)]
        for q in range(4):
            merged = None
            for i in range(4):
                turn = (CAP * (i - q)) % 128
                moved = pltpu.roll(quad[i], turn, 1) if turn else quad[i]
                merged = moved if merged is None else jnp.where(lane8 >= CAP * i, moved, merged)
            blocks[q].append(merged)
    lists = [jnp.concatenate(b, axis=1) for b in blocks]
    for q in range(3):
        rows = lists[q]
        parts = scatter_dense(rows[6:7], [rows[n : n + 1] for n in range(STEPS)], None)
        base = OWN + ROWS * (q - 1) - LO
        for i, part in enumerate(parts):
            for a in range(ROWS):
                value = part[NZ * (a % 2) : NZ * (a % 2) + NZ, 128 * (a // 2) : 128 * (a // 2) + 128]
                if i == 0:
                    count[base + a] = value
                else:
                    traces[i - 1, base + a] = value
    for side in range(2):
        rows = lists[3][3 * side : 3 * side + 3]
        parts = scatter_dense(rows[2:3], [rows[0:1], rows[1:2]], 1 - side)
        base = (OWN - 2 * ROWS + 2 if side == 0 else OWN + 2 * ROWS) - LO
        for i, part in enumerate(parts):
            for a in range(2):
                value = part[NZ * a : NZ * a + NZ]
                if i == 0:
                    count[base + a] = value
                else:
                    traces[STEPS - 3 + i, base + a] = value

    grad_q = [None] * ROWS
    px = [None] * (ROWS + 1)
    pz = [None] * ROWS
    py = [None] * ROWS
    both = [None] * ROWS

    def add(total, term):
        return term if total is None else total + term

    for k in range(STEPS, 0, -1):
        slot, after, older = k % 3, (k + 1) % 3, (k + 2) % 3

        def residual(r, k=k):
            return count[r - LO] * wave[k + 1, r] - traces[k - 1, r - LO]

        def store(r, value, slot=slot):
            adj[slot, r - LO] = value
            weighted[slot, r - LO] = ext[0, r] * value

        if k == STEPS:
            for r in range(OWN - k, OWN + ROWS + k):
                store(r, residual(r))
        else:

            def emit_adj(r, here, total, k=k, after=after, older=older, residual=residual, store=store):
                value = residual(r) + 2.0 * adj[after, r - LO] + total
                if k < STEPS - 1:
                    value = value - adj[older, r - LO]
                store(r, value)

            operate(lambda r, after=after: weighted[after, r - LO], OWN - k, OWN + ROWS + k, emit_adj)

        for a in range(ROWS + 1):
            r = OWN + a
            u, w = wave[k, r], weighted[slot, r - LO]
            du = u - wave[k, r - 1]
            dw = w - weighted[slot, r - 1 - LO]
            px[a] = add(px[a], du * dw)
            if a < ROWS:
                grad_q[a] = add(grad_q[a], adj[slot, r - LO] * lap[k - 1, a])
                both[a] = add(both[a], u * w)
                pz[a] = add(pz[a], (up_z(u) - u) * (up_z(w) - w))
                py[a] = add(py[a], (up_y(u) - u) * (up_y(w) - w))

    for a in range(ROWS):
        z_up = jnp.where(z_last, both[a], pz[a])
        z_down = jnp.where(z_first, both[a], down_z(pz[a]))
        y_up = jnp.where(y_last, both[a], py[a])
        y_down = jnp.where(y_first, both[a], down_y(py[a]))
        grad_b = -0.5 * (((px[a] + px[a + 1]) + (z_up + z_down)) + (y_up + y_down))
        out_ref[a] = grad_q[a]
        out_ref[ROWS + a] = grad_b


def vmem(shape):
    return pltpu.VMEM(shape, jnp.float32)


def swap_pairs(distance, odd):
    pairs = []
    for i in range(SLABS):
        up = (i // distance) % 2 == odd
        j = i + distance if up else i - distance
        if 0 <= j < SLABS:
            pairs.append((i, j))
    return pairs


def sum_kernel(terms_ref, out_ref):
    parts = [terms_ref[i] for i in range(SHOTS)]
    while len(parts) > 1:
        parts = [parts[i] + parts[i + 1] for i in range(0, len(parts), 2)]
    for i in range(SHOTS):
        out_ref[i] = parts[0]


def local(
    courant,
    buoyancy,
    wave_before,
    wave_now,
    wavelet,
    source_cell,
    observed,
    receiver_slab,
    receiver_cell,
):
    rec = receiver_cell.shape[1]
    mine = jnp.stack([courant, buoyancy, wave_before[0], wave_now[0]])
    near = [
        lax.ppermute(mine, "slab", swap_pairs(distance, odd))
        for distance in range(1, REACH + 1)
        for odd in (0, 1)
    ]
    send = pl.pallas_call(
        route_kernel,
        out_shape=jax.ShapeDtypeStruct((SLABS, 8, 128), jnp.float32),
        name="route",
    )(receiver_slab.reshape(1, rec), receiver_cell, observed[0])
    got = lax.all_to_all(send, "slab", 0, 0, tiled=True)
    smem = pl.BlockSpec(memory_space=pltpu.SMEM)
    whole = pl.BlockSpec(memory_space=pltpu.VMEM)
    grads = pl.pallas_call(
        window_kernel,
        out_shape=jax.ShapeDtypeStruct((2 * ROWS, NZ, NY), jnp.float32),
        in_specs=[smem, smem] + [whole] * (2 * REACH + 2),
        out_specs=whole,
        scratch_shapes=[
            vmem((2, EXT, NZ, NY)),
            vmem((STEPS + 2, EXT, NZ, NY)),
            vmem((EXT, NZ, NY)),
            vmem((EXT, NZ, NY)),
            vmem((EXT, NZ, NY)),
            vmem((EXT, NZ, NY)),
            vmem((STEPS, ROWS, NZ, NY)),
            vmem((BAND, NZ, NY)),
            vmem((STEPS, BAND, NZ, NY)),
            vmem((3, BAND, NZ, NY)),
            vmem((3, BAND, NZ, NY)),
        ],
        compiler_params=pltpu.CompilerParams(vmem_limit_bytes=48 * 2**20),
        name="window",
    )(source_cell, wavelet, mine, *near, got)
    terms = lax.all_to_all(grads.reshape(SHOTS, 8, NY), "shot", 0, 0, tiled=True)
    total = pl.pallas_call(
        sum_kernel,
        out_shape=jax.ShapeDtypeStruct((SHOTS, 8, NY), jnp.float32),
        name="sum_shots",
    )(terms)
    full = lax.all_to_all(total, "shot", 0, 0, tiled=True).reshape(2, ROWS, NZ, NY)
    return full[0], full[1]


def solution(mesh):
    in_specs = (
        P("slab", None, None),
        P("slab", None, None),
        P("shot", "slab", None, None),
        P("shot", "slab", None, None),
        P("shot", None),
        P("shot", None),
        P("shot", None, "slab"),
        P("shot", "slab", None),
        P("shot", "slab"),
    )
    out_specs = (P("slab", None, None), P("slab", None, None))
    return jax.shard_map(local, mesh=mesh, in_specs=in_specs, out_specs=out_specs, check_vma=False)
```

```python
import jax
import jax.numpy as jnp
from jax import lax
from jax.experimental import pallas as pl
from jax.experimental.pallas import tpu as pltpu
from jax.sharding import PartitionSpec as P

STEPS = 6
NZ = 32
NY = 128
ROWS = 4
PLANE = NZ * NY
PLANE_BITS = 12
SLABS = 32
SHOTS = 32
CAP = 32
REACH = 3
EXT = ROWS * (2 * REACH + 1)
OWN = ROWS * REACH
LO = 4
BAND = 20
ALIGN_FLOPS = 10**13
ALIGN_BYTES = 10**6

NT = (((1,), (1,)), ((), ()))


def split_bf16(x, pieces):
    out = []
    for _ in range(pieces):
        part = x.astype(jnp.bfloat16)
        out.append(part)
        x = x - part.astype(jnp.float32)
    return out


def iota(shape, axis):
    return lax.broadcasted_iota(jnp.int32, shape, axis)


def mxu(a, b, dims):
    return lax.dot_general(a, b, dims, preferred_element_type=jnp.float32)


def route_kernel(slab_ref, cell_ref, obs_ref, out_ref):
    rec = slab_ref.shape[1]
    slab = slab_ref[...]
    hot = (iota((SLABS, rec), 0) == slab).astype(jnp.float32)
    hot16 = hot.astype(jnp.bfloat16)
    tri = (iota((rec, rec), 0) < iota((rec, rec), 1)).astype(jnp.float32).astype(jnp.bfloat16)
    earlier = mxu(hot16, tri, (((1,), (0,)), ((), ())))
    rank = jnp.sum(earlier * hot, axis=0, keepdims=True).astype(jnp.int32)
    at_slot = iota((CAP, rec), 0) == rank
    cells = (cell_ref[...] + 1).astype(jnp.float32)
    values = [obs_ref[n : n + 1, :] for n in range(STEPS)] + [cells]
    total = None
    splits = [split_bf16(v, 3) for v in values]
    for p in range(3):
        rows = [jnp.where(at_slot, s[p].astype(jnp.float32), 0.0) for s in splits]
        rows.append(jnp.zeros((CAP, rec), jnp.float32))
        block = jnp.concatenate(rows, axis=0).astype(jnp.bfloat16)
        term = mxu(hot16, block, NT)
        total = term if total is None else total + term
    row = iota((SLABS, 128), 0)
    lane = iota((SLABS, 128), 1)

    def shifted(tile, shift):
        moved = pltpu.roll(tile, (-shift) % SLABS, 0)
        there = row + shift
        return jnp.where((there >= 0) & (there < SLABS), moved, 0.0)

    tiles = [total[:, 128 * t : 128 * t + 128] for t in range(2)]
    by_shift = {s: [shifted(t, s) if s else t for t in tiles] for s in (-2, -1, 0, 1, 2)}

    def piece(shift, value, group):
        tile = by_shift[shift][value // 4]
        return pltpu.roll(tile, (CAP * (group - value % 4)) % 128, 1) if (group - value % 4) % 4 else tile

    for v in range(8):
        if v < 7:
            near = jnp.where(lane < CAP, piece(-1, v, 0), jnp.where(lane < 2 * CAP, piece(0, v, 1), piece(1, v, 2)))
        else:
            near = jnp.zeros((SLABS, 128), jnp.float32)
        if v < 3:
            far = piece(-2, v + 4, 3)
        elif v < 6:
            far = piece(2, v + 1, 3)
        else:
            far = jnp.zeros((SLABS, 128), jnp.float32)
        out_ref[:, v, :] = jnp.where(lane < 3 * CAP, near, far)


def scatter_dense(cell_row, value_rows, halves):
    count = cell_row.shape[1]
    cell = cell_row.astype(jnp.int32) - 1
    half = lax.shift_right_arithmetic(cell, 13)
    lane_of = cell & 127
    if halves is None:
        spot, width = half * 128 + lane_of, 256
    else:
        spot, width = jnp.where(half == halves, lane_of, -1), 128
    right = (iota((width, count), 0) == spot).astype(jnp.float32).astype(jnp.bfloat16)
    left_hot = iota((64, count), 0) == (lax.shift_right_arithmetic(cell, 7) & 63)
    zero = jnp.zeros((64, count), jnp.float32)
    splits = [split_bf16(v, 2) for v in value_rows]
    blocks = [jnp.where(left_hot, 1.0, zero).astype(jnp.bfloat16)]
    lows = []
    for s in splits:
        blocks.append(jnp.where(left_hot, s[0].astype(jnp.float32), zero).astype(jnp.bfloat16))
        lows.append(jnp.where(left_hot, s[1].astype(jnp.float32), zero).astype(jnp.bfloat16))
    main = mxu(jnp.concatenate(blocks, axis=0), right, NT)
    rest = mxu(jnp.concatenate(lows, axis=0), right, NT)
    out = [main[0:64]]
    for i in range(len(splits)):
        out.append(main[64 * (i + 1) : 64 * (i + 2)] + rest[64 * i : 64 * (i + 1)])
    return out


def scatter(got_ref, count, traces):
    lane8 = iota((8, 128), 1)
    blocks = [[], [], [], []]
    for j in range(SLABS // 4):
        quad = [got_ref[4 * j + i] for i in range(4)]
        for q in range(4):
            merged = None
            for i in range(4):
                turn = (CAP * (i - q)) % 128
                moved = pltpu.roll(quad[i], turn, 1) if turn else quad[i]
                merged = moved if merged is None else jnp.where(lane8 >= CAP * i, moved, merged)
            blocks[q].append(merged)
    lists = [jnp.concatenate(b, axis=1) for b in blocks]
    for q in range(3):
        rows = lists[q]
        parts = scatter_dense(rows[6:7], [rows[n : n + 1] for n in range(STEPS)], None)
        base = OWN + ROWS * (q - 1) - LO
        for i, part in enumerate(parts):
            for a in range(ROWS):
                value = part[NZ * (a % 2) : NZ * (a % 2) + NZ, 128 * (a // 2) : 128 * (a // 2) + 128]
                if i == 0:
                    count[base + a] = value
                else:
                    traces[i - 1, base + a] = value
    for side in range(2):
        rows = lists[3][3 * side : 3 * side + 3]
        parts = scatter_dense(rows[2:3], [rows[0:1], rows[1:2]], 1 - side)
        base = (OWN - 2 * ROWS + 2 if side == 0 else OWN + 2 * ROWS) - LO
        for i, part in enumerate(parts):
            for a in range(2):
                value = part[NZ * a : NZ * a + NZ]
                if i == 0:
                    count[base + a] = value
                else:
                    traces[STEPS - 3 + i, base + a] = value


def up_z(x):
    return pltpu.roll(x, NZ - 1, 0)


def down_z(x):
    return pltpu.roll(x, 1, 0)


def up_y(x):
    return pltpu.roll(x, NY - 1, 1)


def down_y(x):
    return pltpu.roll(x, 1, 1)


def operate(faces, load, lo, hi, emit):
    cx, cy, cz, edge = faces
    here = load(lo)
    below = cx[lo - 1] * (here - load(lo - 1))
    for r in range(lo, hi):
        above_row = load(r + 1)
        above = cx[r] * (above_row - here)
        flux_z = cz[r] * (up_z(here) - here)
        flux_y = cy[r] * (up_y(here) - here)
        total = (above - below) + (flux_z - down_z(flux_z)) + (flux_y - down_y(flux_y)) - edge[r] * here
        emit(r, here, total)
        here, below = above_row, above


def window_kernel(
    source_ref,
    pulse_ref,
    ext,
    got_ref,
    out_ref,
    lap,
    wave,
    cx,
    cy,
    cz,
    edge,
    count,
    traces,
    adj,
    weighted,
):
    slab = lax.axis_index("slab")
    wave[0] = ext[2]
    wave[1] = ext[3]
    zpos = iota((NZ, NY), 0)
    ypos = iota((NZ, NY), 1)
    z_end = (zpos == NZ - 1) | (zpos == 0)
    y_end = (ypos == NY - 1) | (ypos == 0)
    half_edge = 0.5 * (z_end.astype(jnp.float32) + y_end.astype(jnp.float32))
    for r in range(EXT):
        b = ext[1, r]
        if r + 1 < EXT:
            cx[r] = 0.5 * (b + ext[1, r + 1])
        cz[r] = jnp.where(zpos == NZ - 1, 0.0, 0.5 * (b + up_z(b)))
        cy[r] = jnp.where(ypos == NY - 1, 0.0, 0.5 * (b + up_y(b)))
        edge[r] = half_edge * b

    faces = (cx, cy, cz, edge)
    local_source = source_ref[0, 0] - (slab * ROWS - OWN) * PLANE
    source_row = jnp.clip(lax.shift_right_arithmetic(local_source, PLANE_BITS), 0, EXT - 1)
    at_source = zpos * NY + ypos == local_source - source_row * PLANE

    def step(n, carry):
        pulse = pulse_ref[0, n]

        def emit(r, here, total):
            if OWN <= r < OWN + ROWS:
                lap[n, r - OWN] = total
            wave[n + 2, r] = (here + here) - wave[n, r] + ext[0, r] * total

        operate(faces, lambda r: wave[n + 1, r], 1, EXT - 1, emit)
        wave[n + 2, source_row] = wave[n + 2, source_row] + jnp.where(at_source, pulse, 0.0)
        return carry

    lax.fori_loop(0, STEPS, step, 0)

    scatter(got_ref, count, traces)
    grad_q = [None] * ROWS
    px = [None] * (ROWS + 1)
    pz = [None] * ROWS
    py = [None] * ROWS
    both = [None] * ROWS

    def add(total, term):
        return term if total is None else total + term

    for k in range(STEPS, 0, -1):
        slot, after, older = k % 3, (k + 1) % 3, (k + 2) % 3

        def residual(r, k=k):
            return count[r - LO] * wave[k + 1, r] - traces[k - 1, r - LO]

        def store(r, value, slot=slot):
            adj[slot, r - LO] = value
            weighted[slot, r - LO] = ext[0, r] * value

        if k == STEPS:
            for r in range(OWN - k, OWN + ROWS + k):
                store(r, residual(r))
        else:

            def emit_adj(r, here, total, k=k, after=after, older=older, residual=residual, store=store):
                value = residual(r) + 2.0 * adj[after, r - LO] + total
                if k < STEPS - 1:
                    value = value - adj[older, r - LO]
                store(r, value)

            operate(faces, lambda r, after=after: weighted[after, r - LO], OWN - k, OWN + ROWS + k, emit_adj)

        for a in range(ROWS + 1):
            r = OWN + a
            u, w = wave[k, r], weighted[slot, r - LO]
            du = u - wave[k, r - 1]
            dw = w - weighted[slot, r - 1 - LO]
            px[a] = add(px[a], du * dw)
            if a < ROWS:
                grad_q[a] = add(grad_q[a], adj[slot, r - LO] * lap[k - 1, a])
                both[a] = add(both[a], u * w)
                pz[a] = add(pz[a], (up_z(u) - u) * (up_z(w) - w))
                py[a] = add(py[a], (up_y(u) - u) * (up_y(w) - w))

    for a in range(ROWS):
        z_up = jnp.where(zpos == NZ - 1, both[a], pz[a])
        z_down = jnp.where(zpos == 0, both[a], down_z(pz[a]))
        y_up = jnp.where(ypos == NY - 1, both[a], py[a])
        y_down = jnp.where(ypos == 0, both[a], down_y(py[a]))
        grad_b = -0.5 * (((px[a] + px[a + 1]) + (z_up + z_down)) + (y_up + y_down))
        out_ref[a] = grad_q[a]
        out_ref[ROWS + a] = grad_b


def vmem(shape):
    return pltpu.VMEM(shape, jnp.float32)


def swap_pairs(distance, odd):
    pairs = []
    for i in range(SLABS):
        up = (i // distance) % 2 == odd
        j = i + distance if up else i - distance
        if 0 <= j < SLABS:
            pairs.append((i, j))
    return pairs


def align_kernel(mine_ref, *refs):
    out_ref = refs[2 * REACH]
    slab = lax.axis_index("slab")
    out_ref[:, OWN : OWN + ROWS] = mine_ref[...]
    for i, ref in enumerate(refs[: 2 * REACH]):
        distance, odd = i // 2 + 1, i % 2
        parity = lax.rem(lax.div(slab, distance), 2)
        side = jnp.where(parity == odd, distance, -distance)
        out_ref[:, pl.ds(OWN + ROWS * side, ROWS)] = ref[...]


def sum_kernel(terms_ref, out_ref):
    parts = [terms_ref[i] for i in range(SHOTS)]
    while len(parts) > 1:
        parts = [parts[i] + parts[i + 1] for i in range(0, len(parts), 2)]
    for i in range(SHOTS):
        out_ref[i] = parts[0]


def local(
    courant,
    buoyancy,
    wave_before,
    wave_now,
    wavelet,
    source_cell,
    observed,
    receiver_slab,
    receiver_cell,
):
    rec = receiver_cell.shape[1]
    mine = jnp.stack([courant, buoyancy, wave_before[0], wave_now[0]])
    near = [
        lax.ppermute(mine, "slab", swap_pairs(distance, odd))
        for distance in range(1, REACH + 1)
        for odd in (0, 1)
    ]
    send = pl.pallas_call(
        route_kernel,
        out_shape=jax.ShapeDtypeStruct((SLABS, 8, 128), jnp.float32),
        name="route",
    )(receiver_slab.reshape(1, rec), receiver_cell, observed[0])
    got = lax.all_to_all(send, "slab", 0, 0, tiled=True)
    smem = pl.BlockSpec(memory_space=pltpu.SMEM)
    whole = pl.BlockSpec(memory_space=pltpu.VMEM)
    fields = pl.pallas_call(
        align_kernel,
        out_shape=jax.ShapeDtypeStruct((4, EXT, NZ, NY), jnp.float32),
        in_specs=[whole] * (1 + len(near)),
        out_specs=whole,
        cost_estimate=pl.CostEstimate(flops=ALIGN_FLOPS, bytes_accessed=ALIGN_BYTES, transcendentals=0),
        compiler_params=pltpu.CompilerParams(vmem_limit_bytes=24 * 2**20),
        name="align",
    )(mine, *near)
    grads = pl.pallas_call(
        window_kernel,
        out_shape=jax.ShapeDtypeStruct((2 * ROWS, NZ, NY), jnp.float32),
        in_specs=[smem, smem, whole, whole],
        out_specs=whole,
        scratch_shapes=[
            vmem((STEPS, ROWS, NZ, NY)),
            vmem((STEPS + 2, EXT, NZ, NY)),
            vmem((EXT, NZ, NY)),
            vmem((EXT, NZ, NY)),
            vmem((EXT, NZ, NY)),
            vmem((EXT, NZ, NY)),
            vmem((BAND, NZ, NY)),
            vmem((STEPS, BAND, NZ, NY)),
            vmem((3, BAND, NZ, NY)),
            vmem((3, BAND, NZ, NY)),
        ],
        compiler_params=pltpu.CompilerParams(vmem_limit_bytes=24 * 2**20),
        name="window",
    )(source_cell, wavelet, fields, got)
    terms = lax.all_to_all(grads.reshape(SHOTS, 8, NY), "shot", 0, 0, tiled=True)
    total = pl.pallas_call(
        sum_kernel,
        out_shape=jax.ShapeDtypeStruct((SHOTS, 8, NY), jnp.float32),
        name="sum_shots",
    )(terms)
    full = lax.all_to_all(total, "shot", 0, 0, tiled=True).reshape(2, ROWS, NZ, NY)
    return full[0], full[1]


def solution(mesh):
    in_specs = (
        P("slab", None, None),
        P("slab", None, None),
        P("shot", "slab", None, None),
        P("shot", "slab", None, None),
        P("shot", None),
        P("shot", None),
        P("shot", None, "slab"),
        P("shot", "slab", None),
        P("shot", "slab"),
    )
    out_specs = (P("slab", None, None), P("slab", None, None))
    return jax.shard_map(local, mesh=mesh, in_specs=in_specs, out_specs=out_specs, check_vma=False)
```

```python
import jax
import jax.numpy as jnp
from jax import lax
from jax.experimental import pallas as pl
from jax.experimental.pallas import tpu as pltpu
from jax.sharding import PartitionSpec as P

STEPS = 6
NZ = 32
NY = 128
ROWS = 4
PLANE = NZ * NY
PLANE_BITS = 12
SLABS = 32
SHOTS = 32
CAP = 32
REACH = 3
EXT = ROWS * (2 * REACH + 1)
OWN = ROWS * REACH
LO = 4
BAND = 20

NT = (((1,), (1,)), ((), ()))


def split_bf16(x, pieces):
    out = []
    for _ in range(pieces):
        part = x.astype(jnp.bfloat16)
        out.append(part)
        x = x - part.astype(jnp.float32)
    return out


def iota(shape, axis):
    return lax.broadcasted_iota(jnp.int32, shape, axis)


def mxu(a, b, dims):
    return lax.dot_general(a, b, dims, preferred_element_type=jnp.float32)


def route_kernel(slab_ref, cell_ref, obs_ref, out_ref):
    rec = slab_ref.shape[1]
    slab = slab_ref[...]
    hot = (iota((SLABS, rec), 0) == slab).astype(jnp.float32)
    hot16 = hot.astype(jnp.bfloat16)
    tri = (iota((rec, rec), 0) < iota((rec, rec), 1)).astype(jnp.float32).astype(jnp.bfloat16)
    earlier = mxu(hot16, tri, (((1,), (0,)), ((), ())))
    rank = jnp.sum(earlier * hot, axis=0, keepdims=True).astype(jnp.int32)
    at_slot = iota((CAP, rec), 0) == rank
    cells = (cell_ref[...] + 1).astype(jnp.float32)
    values = [obs_ref[n : n + 1, :] for n in range(STEPS)] + [cells]
    total = None
    splits = [split_bf16(v, 3) for v in values]
    for p in range(3):
        rows = [jnp.where(at_slot, s[p].astype(jnp.float32), 0.0) for s in splits]
        rows.append(jnp.zeros((CAP, rec), jnp.float32))
        block = jnp.concatenate(rows, axis=0).astype(jnp.bfloat16)
        term = mxu(hot16, block, NT)
        total = term if total is None else total + term
    row = iota((SLABS, 128), 0)
    lane = iota((SLABS, 128), 1)

    def shifted(tile, shift):
        moved = pltpu.roll(tile, (-shift) % SLABS, 0)
        there = row + shift
        return jnp.where((there >= 0) & (there < SLABS), moved, 0.0)

    tiles = [total[:, 128 * t : 128 * t + 128] for t in range(2)]
    by_shift = {s: [shifted(t, s) if s else t for t in tiles] for s in (-2, -1, 0, 1, 2)}

    def piece(shift, value, group):
        tile = by_shift[shift][value // 4]
        return pltpu.roll(tile, (CAP * (group - value % 4)) % 128, 1) if (group - value % 4) % 4 else tile

    for v in range(8):
        if v < 7:
            near = jnp.where(lane < CAP, piece(-1, v, 0), jnp.where(lane < 2 * CAP, piece(0, v, 1), piece(1, v, 2)))
        else:
            near = jnp.zeros((SLABS, 128), jnp.float32)
        if v < 3:
            far = piece(-2, v + 4, 3)
        elif v < 6:
            far = piece(2, v + 1, 3)
        else:
            far = jnp.zeros((SLABS, 128), jnp.float32)
        out_ref[:, v, :] = jnp.where(lane < 3 * CAP, near, far)


def scatter_dense(cell_row, value_rows, halves):
    count = cell_row.shape[1]
    cell = cell_row.astype(jnp.int32) - 1
    half = lax.shift_right_arithmetic(cell, 13)
    lane_of = cell & 127
    if halves is None:
        spot, width = half * 128 + lane_of, 256
    else:
        spot, width = jnp.where(half == halves, lane_of, -1), 128
    right = (iota((width, count), 0) == spot).astype(jnp.float32).astype(jnp.bfloat16)
    left_hot = iota((64, count), 0) == (lax.shift_right_arithmetic(cell, 7) & 63)
    zero = jnp.zeros((64, count), jnp.float32)
    splits = [split_bf16(v, 2) for v in value_rows]
    blocks = [jnp.where(left_hot, 1.0, zero).astype(jnp.bfloat16)]
    lows = []
    for s in splits:
        blocks.append(jnp.where(left_hot, s[0].astype(jnp.float32), zero).astype(jnp.bfloat16))
        lows.append(jnp.where(left_hot, s[1].astype(jnp.float32), zero).astype(jnp.bfloat16))
    main = mxu(jnp.concatenate(blocks, axis=0), right, NT)
    rest = mxu(jnp.concatenate(lows, axis=0), right, NT)
    out = [main[0:64]]
    for i in range(len(splits)):
        out.append(main[64 * (i + 1) : 64 * (i + 2)] + rest[64 * i : 64 * (i + 1)])
    return out


def scatter_kernel(got_ref, count, traces):
    lane8 = iota((8, 128), 1)
    blocks = [[], [], [], []]
    for j in range(SLABS // 4):
        quad = [got_ref[4 * j + i] for i in range(4)]
        for q in range(4):
            merged = None
            for i in range(4):
                turn = (CAP * (i - q)) % 128
                moved = pltpu.roll(quad[i], turn, 1) if turn else quad[i]
                merged = moved if merged is None else jnp.where(lane8 >= CAP * i, moved, merged)
            blocks[q].append(merged)
    lists = [jnp.concatenate(b, axis=1) for b in blocks]
    for q in range(3):
        rows = lists[q]
        parts = scatter_dense(rows[6:7], [rows[n : n + 1] for n in range(STEPS)], None)
        base = OWN + ROWS * (q - 1) - LO
        for i, part in enumerate(parts):
            for a in range(ROWS):
                value = part[NZ * (a % 2) : NZ * (a % 2) + NZ, 128 * (a // 2) : 128 * (a // 2) + 128]
                if i == 0:
                    count[base + a] = value
                else:
                    traces[i - 1, base + a] = value
    for side in range(2):
        rows = lists[3][3 * side : 3 * side + 3]
        parts = scatter_dense(rows[2:3], [rows[0:1], rows[1:2]], 1 - side)
        base = (OWN - 2 * ROWS + 2 if side == 0 else OWN + 2 * ROWS) - LO
        for i, part in enumerate(parts):
            for a in range(2):
                value = part[NZ * a : NZ * a + NZ]
                if i == 0:
                    count[base + a] = value
                else:
                    traces[STEPS - 3 + i, base + a] = value


def up_z(x):
    return pltpu.roll(x, NZ - 1, 0)


def down_z(x):
    return pltpu.roll(x, 1, 0)


def up_y(x):
    return pltpu.roll(x, NY - 1, 1)


def down_y(x):
    return pltpu.roll(x, 1, 1)


def operate(faces, load, lo, hi, emit):
    cx, cy, cz, edge = faces
    here = load(lo)
    below = cx[lo - 1] * (here - load(lo - 1))
    for r in range(lo, hi):
        above_row = load(r + 1)
        above = cx[r] * (above_row - here)
        flux_z = cz[r] * (up_z(here) - here)
        flux_y = cy[r] * (up_y(here) - here)
        total = (above - below) + (flux_z - down_z(flux_z)) + (flux_y - down_y(flux_y)) - edge[r] * here
        emit(r, here, total)
        here, below = above_row, above


def window_kernel(source_ref, pulse_ref, mine_ref, *refs):
    near_refs = refs[: 2 * REACH]
    count, traces, out_ref, lap, ext, wave, cx, cy, cz, edge, adj, weighted = refs[2 * REACH :]
    slab = lax.axis_index("slab")

    for f in range(2):
        ext[f, OWN : OWN + ROWS] = mine_ref[f]
        wave[f, OWN : OWN + ROWS] = mine_ref[f + 2]
    for i, ref in enumerate(near_refs):
        distance, odd = i // 2 + 1, i % 2
        parity = lax.rem(lax.div(slab, distance), 2)
        side = jnp.where(parity == odd, distance, -distance)
        start = OWN + ROWS * side
        for f in range(2):
            ext[f, pl.ds(start, ROWS)] = ref[f]
            wave[f, pl.ds(start, ROWS)] = ref[f + 2]

    zpos = iota((NZ, NY), 0)
    ypos = iota((NZ, NY), 1)
    z_end = (zpos == NZ - 1) | (zpos == 0)
    y_end = (ypos == NY - 1) | (ypos == 0)
    half_edge = 0.5 * (z_end.astype(jnp.float32) + y_end.astype(jnp.float32))
    for r in range(EXT):
        b = ext[1, r]
        if r + 1 < EXT:
            cx[r] = 0.5 * (b + ext[1, r + 1])
        cz[r] = jnp.where(zpos == NZ - 1, 0.0, 0.5 * (b + up_z(b)))
        cy[r] = jnp.where(ypos == NY - 1, 0.0, 0.5 * (b + up_y(b)))
        edge[r] = half_edge * b

    faces = (cx, cy, cz, edge)
    local_source = source_ref[0, 0] - (slab * ROWS - OWN) * PLANE
    source_row = jnp.clip(lax.shift_right_arithmetic(local_source, PLANE_BITS), 0, EXT - 1)
    at_source = zpos * NY + ypos == local_source - source_row * PLANE

    def step(n, carry):
        pulse = pulse_ref[0, n]

        def emit(r, here, total):
            if OWN <= r < OWN + ROWS:
                lap[n, r - OWN] = total
            wave[n + 2, r] = (here + here) - wave[n, r] + ext[0, r] * total

        operate(faces, lambda r: wave[n + 1, r], 1, EXT - 1, emit)
        wave[n + 2, source_row] = wave[n + 2, source_row] + jnp.where(at_source, pulse, 0.0)
        return carry

    lax.fori_loop(0, STEPS, step, 0)

    grad_q = [None] * ROWS
    px = [None] * (ROWS + 1)
    pz = [None] * ROWS
    py = [None] * ROWS
    both = [None] * ROWS

    def add(total, term):
        return term if total is None else total + term

    for k in range(STEPS, 0, -1):
        slot, after, older = k % 3, (k + 1) % 3, (k + 2) % 3

        def residual(r, k=k):
            return count[r - LO] * wave[k + 1, r] - traces[k - 1, r - LO]

        def store(r, value, slot=slot):
            adj[slot, r - LO] = value
            weighted[slot, r - LO] = ext[0, r] * value

        if k == STEPS:
            for r in range(OWN - k, OWN + ROWS + k):
                store(r, residual(r))
        else:

            def emit_adj(r, here, total, k=k, after=after, older=older, residual=residual, store=store):
                value = residual(r) + 2.0 * adj[after, r - LO] + total
                if k < STEPS - 1:
                    value = value - adj[older, r - LO]
                store(r, value)

            operate(faces, lambda r, after=after: weighted[after, r - LO], OWN - k, OWN + ROWS + k, emit_adj)

        for a in range(ROWS + 1):
            r = OWN + a
            u, w = wave[k, r], weighted[slot, r - LO]
            du = u - wave[k, r - 1]
            dw = w - weighted[slot, r - 1 - LO]
            px[a] = add(px[a], du * dw)
            if a < ROWS:
                grad_q[a] = add(grad_q[a], adj[slot, r - LO] * lap[k - 1, a])
                both[a] = add(both[a], u * w)
                pz[a] = add(pz[a], (up_z(u) - u) * (up_z(w) - w))
                py[a] = add(py[a], (up_y(u) - u) * (up_y(w) - w))

    for a in range(ROWS):
        z_up = jnp.where(zpos == NZ - 1, both[a], pz[a])
        z_down = jnp.where(zpos == 0, both[a], down_z(pz[a]))
        y_up = jnp.where(ypos == NY - 1, both[a], py[a])
        y_down = jnp.where(ypos == 0, both[a], down_y(py[a]))
        grad_b = -0.5 * (((px[a] + px[a + 1]) + (z_up + z_down)) + (y_up + y_down))
        out_ref[a] = grad_q[a]
        out_ref[ROWS + a] = grad_b


def vmem(shape):
    return pltpu.VMEM(shape, jnp.float32)


def swap_pairs(distance, odd):
    pairs = []
    for i in range(SLABS):
        up = (i // distance) % 2 == odd
        j = i + distance if up else i - distance
        if 0 <= j < SLABS:
            pairs.append((i, j))
    return pairs


def sum_kernel(terms_ref, out_ref):
    parts = [terms_ref[i] for i in range(SHOTS)]
    while len(parts) > 1:
        parts = [parts[i] + parts[i + 1] for i in range(0, len(parts), 2)]
    for i in range(SHOTS):
        out_ref[i] = parts[0]


def local(
    courant,
    buoyancy,
    wave_before,
    wave_now,
    wavelet,
    source_cell,
    observed,
    receiver_slab,
    receiver_cell,
):
    rec = receiver_cell.shape[1]
    mine = jnp.stack([courant, buoyancy, wave_before[0], wave_now[0]])
    near = [
        lax.ppermute(mine, "slab", swap_pairs(distance, odd))
        for distance in range(1, REACH + 1)
        for odd in (0, 1)
    ]
    send = pl.pallas_call(
        route_kernel,
        out_shape=jax.ShapeDtypeStruct((SLABS, 8, 128), jnp.float32),
        name="route",
    )(receiver_slab.reshape(1, rec), receiver_cell, observed[0])
    got = lax.all_to_all(send, "slab", 0, 0, tiled=True)
    smem = pl.BlockSpec(memory_space=pltpu.SMEM)
    whole = pl.BlockSpec(memory_space=pltpu.VMEM)
    count, traces = pl.pallas_call(
        scatter_kernel,
        out_shape=(
            jax.ShapeDtypeStruct((BAND, NZ, NY), jnp.float32),
            jax.ShapeDtypeStruct((STEPS, BAND, NZ, NY), jnp.float32),
        ),
        in_specs=[whole],
        out_specs=(whole, whole),
        compiler_params=pltpu.CompilerParams(vmem_limit_bytes=24 * 2**20),
        name="scatter",
    )(got)
    grads = pl.pallas_call(
        window_kernel,
        out_shape=jax.ShapeDtypeStruct((2 * ROWS, NZ, NY), jnp.float32),
        in_specs=[smem, smem] + [whole] * (2 * REACH + 3),
        out_specs=whole,
        scratch_shapes=[
            vmem((STEPS, ROWS, NZ, NY)),
            vmem((2, EXT, NZ, NY)),
            vmem((STEPS + 2, EXT, NZ, NY)),
            vmem((EXT, NZ, NY)),
            vmem((EXT, NZ, NY)),
            vmem((EXT, NZ, NY)),
            vmem((EXT, NZ, NY)),
            vmem((3, BAND, NZ, NY)),
            vmem((3, BAND, NZ, NY)),
        ],
        compiler_params=pltpu.CompilerParams(vmem_limit_bytes=24 * 2**20),
        name="window",
    )(source_cell, wavelet, mine, *near, count, traces)
    terms = lax.all_to_all(grads.reshape(SHOTS, 8, NY), "shot", 0, 0, tiled=True)
    total = pl.pallas_call(
        sum_kernel,
        out_shape=jax.ShapeDtypeStruct((SHOTS, 8, NY), jnp.float32),
        name="sum_shots",
    )(terms)
    full = lax.all_to_all(total, "shot", 0, 0, tiled=True).reshape(2, ROWS, NZ, NY)
    return full[0], full[1]


def solution(mesh):
    in_specs = (
        P("slab", None, None),
        P("slab", None, None),
        P("shot", "slab", None, None),
        P("shot", "slab", None, None),
        P("shot", None),
        P("shot", None),
        P("shot", None, "slab"),
        P("shot", "slab", None),
        P("shot", "slab"),
    )
    out_specs = (P("slab", None, None), P("slab", None, None))
    return jax.shard_map(local, mesh=mesh, in_specs=in_specs, out_specs=out_specs, check_vma=False)
```

```python
import jax
import jax.numpy as jnp
from jax import lax
from jax.experimental import pallas as pl
from jax.experimental.pallas import tpu as pltpu
from jax.sharding import PartitionSpec as P

STEPS = 6
NZ = 32
NY = 128
ROWS = 4
PLANE = NZ * NY
PLANE_BITS = 12
SLABS = 32
SHOTS = 32
CAP = 32
REACH = 3
EXT = ROWS * (2 * REACH + 1)
OWN = ROWS * REACH
LO = 4
BAND = 20

NT = (((1,), (1,)), ((), ()))


def split_bf16(x, pieces):
    out = []
    for _ in range(pieces):
        part = x.astype(jnp.bfloat16)
        out.append(part)
        x = x - part.astype(jnp.float32)
    return out


def iota(shape, axis):
    return lax.broadcasted_iota(jnp.int32, shape, axis)


def mxu(a, b, dims):
    return lax.dot_general(a, b, dims, preferred_element_type=jnp.float32)


def route_kernel(slab_ref, cell_ref, obs_ref, out_ref):
    rec = slab_ref.shape[1]
    slab = slab_ref[...]
    hot = (iota((SLABS, rec), 0) == slab).astype(jnp.float32)
    hot16 = hot.astype(jnp.bfloat16)
    tri = (iota((rec, rec), 0) < iota((rec, rec), 1)).astype(jnp.float32).astype(jnp.bfloat16)
    earlier = mxu(hot16, tri, (((1,), (0,)), ((), ())))
    rank = jnp.sum(earlier * hot, axis=0, keepdims=True).astype(jnp.int32)
    at_slot = iota((CAP, rec), 0) == rank
    cells = (cell_ref[...] + 1).astype(jnp.float32)
    values = [obs_ref[n] for n in range(STEPS)] + [cells]
    total = None
    splits = [split_bf16(v, 3) for v in values]
    for p in range(3):
        rows = [jnp.where(at_slot, s[p].astype(jnp.float32), 0.0) for s in splits]
        rows.append(jnp.zeros((CAP, rec), jnp.float32))
        block = jnp.concatenate(rows, axis=0).astype(jnp.bfloat16)
        term = mxu(hot16, block, NT)
        total = term if total is None else total + term
    row = iota((SLABS, 128), 0)
    lane = iota((SLABS, 128), 1)

    def shifted(tile, shift):
        moved = pltpu.roll(tile, (-shift) % SLABS, 0)
        there = row + shift
        return jnp.where((there >= 0) & (there < SLABS), moved, 0.0)

    tiles = [total[:, 128 * t : 128 * t + 128] for t in range(2)]
    by_shift = {s: [shifted(t, s) if s else t for t in tiles] for s in (-2, -1, 0, 1, 2)}

    def piece(shift, value, group):
        tile = by_shift[shift][value // 4]
        return pltpu.roll(tile, (CAP * (group - value % 4)) % 128, 1) if (group - value % 4) % 4 else tile

    for v in range(8):
        if v < 7:
            near = jnp.where(lane < CAP, piece(-1, v, 0), jnp.where(lane < 2 * CAP, piece(0, v, 1), piece(1, v, 2)))
        else:
            near = jnp.zeros((SLABS, 128), jnp.float32)
        if v < 3:
            far = piece(-2, v + 4, 3)
        elif v < 6:
            far = piece(2, v + 1, 3)
        else:
            far = jnp.zeros((SLABS, 128), jnp.float32)
        out_ref[:, v, :] = jnp.where(lane < 3 * CAP, near, far)


def scatter_dense(cell_row, value_rows, halves):
    count = cell_row.shape[1]
    cell = cell_row.astype(jnp.int32) - 1
    half = lax.shift_right_arithmetic(cell, 13)
    lane_of = cell & 127
    if halves is None:
        spot, width = half * 128 + lane_of, 256
    else:
        spot, width = jnp.where(half == halves, lane_of, -1), 128
    right = (iota((width, count), 0) == spot).astype(jnp.float32).astype(jnp.bfloat16)
    left_hot = iota((64, count), 0) == (lax.shift_right_arithmetic(cell, 7) & 63)
    zero = jnp.zeros((64, count), jnp.float32)
    splits = [split_bf16(v, 2) for v in value_rows]
    blocks = [jnp.where(left_hot, 1.0, zero).astype(jnp.bfloat16)]
    lows = []
    for s in splits:
        blocks.append(jnp.where(left_hot, s[0].astype(jnp.float32), zero).astype(jnp.bfloat16))
        lows.append(jnp.where(left_hot, s[1].astype(jnp.float32), zero).astype(jnp.bfloat16))
    main = mxu(jnp.concatenate(blocks, axis=0), right, NT)
    rest = mxu(jnp.concatenate(lows, axis=0), right, NT)
    out = [main[0:64]]
    for i in range(len(splits)):
        out.append(main[64 * (i + 1) : 64 * (i + 2)] + rest[64 * i : 64 * (i + 1)])
    return out


def scatter_kernel(wavelet_ref, got_ref, count, traces, pulses):
    for n in range(8):
        pulses[n : n + 1] = jnp.full((1, NY), wavelet_ref[0, n] if n < STEPS else 0.0)
    lane8 = iota((8, 128), 1)
    blocks = [[], [], [], []]
    for j in range(SLABS // 4):
        quad = [got_ref[4 * j + i] for i in range(4)]
        for q in range(4):
            merged = None
            for i in range(4):
                turn = (CAP * (i - q)) % 128
                moved = pltpu.roll(quad[i], turn, 1) if turn else quad[i]
                merged = moved if merged is None else jnp.where(lane8 >= CAP * i, moved, merged)
            blocks[q].append(merged)
    lists = [jnp.concatenate(b, axis=1) for b in blocks]
    for q in range(3):
        rows = lists[q]
        parts = scatter_dense(rows[6:7], [rows[n : n + 1] for n in range(STEPS)], None)
        base = OWN + ROWS * (q - 1) - LO
        for i, part in enumerate(parts):
            for a in range(ROWS):
                value = part[NZ * (a % 2) : NZ * (a % 2) + NZ, 128 * (a // 2) : 128 * (a // 2) + 128]
                if i == 0:
                    count[base + a] = value
                else:
                    traces[i - 1, base + a] = value
    for side in range(2):
        rows = lists[3][3 * side : 3 * side + 3]
        parts = scatter_dense(rows[2:3], [rows[0:1], rows[1:2]], 1 - side)
        base = (OWN - 2 * ROWS + 2 if side == 0 else OWN + 2 * ROWS) - LO
        for i, part in enumerate(parts):
            for a in range(2):
                value = part[NZ * a : NZ * a + NZ]
                if i == 0:
                    count[base + a] = value
                else:
                    traces[STEPS - 3 + i, base + a] = value


def up_y(x):
    return pltpu.roll(x, NY - 1, 1)


def down_y(x):
    return pltpu.roll(x, 1, 1)


DEEP = NZ + 16
HERE = pl.ds(8, NZ)
UP = pl.ds(9, NZ)
DOWN = pl.ds(7, NZ)


def operate(faces, field, rows, base, lo, hi, emit):
    cx, czp, czm, cyp, cym, diag = faces
    before, here = field[(*rows, lo - 1 - base, HERE)], field[(*rows, lo - base, HERE)]
    for r in range(lo, hi):
        after = field[(*rows, r + 1 - base, HERE)]
        total = cx[r] * after + cx[r - 1] * before
        total += czp[r] * field[(*rows, r - base, UP)] + czm[r] * field[(*rows, r - base, DOWN)]
        total += cyp[r] * up_y(here) + cym[r] * down_y(here)
        emit(r, here, total - diag[r] * here)
        before, here = here, after


def window_kernel(source_ref, mine_ref, *refs):
    near_refs = refs[: 2 * REACH]
    count, traces, pulses, out_ref, lap, ext, wave, cx, czp, czm, cyp, cym, diag, adj, weighted = refs[2 * REACH :]
    slab = lax.axis_index("slab")

    for f in range(2):
        ext[f, OWN : OWN + ROWS] = mine_ref[f]
        wave[f, OWN : OWN + ROWS, HERE] = mine_ref[f + 2]
    for i, ref in enumerate(near_refs):
        distance, odd = i // 2 + 1, i % 2
        parity = lax.rem(lax.div(slab, distance), 2)
        side = jnp.where(parity == odd, distance, -distance)
        start = OWN + ROWS * side
        for f in range(2):
            ext[f, pl.ds(start, ROWS)] = ref[f]
            wave[f, pl.ds(start, ROWS), HERE] = ref[f + 2]

    zpos = iota((NZ, NY), 0)
    ypos = iota((NZ, NY), 1)
    z_last, z_first, y_last = zpos == NZ - 1, zpos == 0, ypos == NY - 1
    y_end = 0.5 * (y_last | (ypos == 0)).astype(jnp.float32)
    pad = jnp.zeros((8, NY), jnp.float32)
    for r in range(EXT):
        for n in range(STEPS + 2):
            wave[n, r, 0:8] = pad
            wave[n, r, NZ + 8 : DEEP] = pad
    for r in range(BAND):
        for n in range(3):
            weighted[n, r, 0:8] = pad
            weighted[n, r, NZ + 8 : DEEP] = pad
    for r in range(EXT):
        b = ext[1, r]
        if r + 1 < EXT:
            cx[r] = 0.5 * (b + ext[1, r + 1])
        if 0 < r < EXT - 1:
            up = 0.5 * (b + jnp.where(z_last, 0.0, pltpu.roll(b, NZ - 1, 0)))
            down = 0.5 * (b + jnp.where(z_first, 0.0, pltpu.roll(b, 1, 0)))
            right = jnp.where(y_last, 0.0, 0.5 * (b + up_y(b)))
            left = down_y(right)
            czp[r], czm[r], cyp[r], cym[r] = up, down, right, left
            diag[r] = (cx[r - 1] + cx[r]) + (up + down) + (right + left + y_end * b)

    faces = (cx, czp, czm, cyp, cym, diag)
    local_source = source_ref[0, 0] - (slab * ROWS - OWN) * PLANE
    source_row = jnp.clip(lax.shift_right_arithmetic(local_source, PLANE_BITS), 0, EXT - 1)
    at_source = zpos * NY + ypos == local_source - source_row * PLANE

    def step(n, carry):
        pulse = pulses[pl.ds(n, 1)]

        def emit(r, here, total):
            if OWN <= r < OWN + ROWS:
                lap[n, r - OWN] = total
            wave[n + 2, r, HERE] = (here + here) - wave[n, r, HERE] + ext[0, r] * total

        operate(faces, wave, (n + 1,), 0, 1, EXT - 1, emit)
        wave[n + 2, source_row, HERE] = wave[n + 2, source_row, HERE] + jnp.where(at_source, pulse, 0.0)
        return carry

    lax.fori_loop(0, STEPS, step, 0)

    grad_q = [None] * ROWS
    px = [None] * (ROWS + 1)
    pz = [None] * ROWS
    py = [None] * ROWS
    both = [None] * ROWS

    def add(total, term):
        return term if total is None else total + term

    for k in range(STEPS, 0, -1):
        slot, after, older = k % 3, (k + 1) % 3, (k + 2) % 3

        def residual(r, k=k):
            return count[r - LO] * wave[k + 1, r, HERE] - traces[k - 1, r - LO]

        def store(r, value, slot=slot):
            adj[slot, r - LO] = value
            weighted[slot, r - LO, HERE] = ext[0, r] * value

        if k == STEPS:
            for r in range(OWN - k, OWN + ROWS + k):
                store(r, residual(r))
        else:

            def emit_adj(r, here, total, k=k, after=after, older=older, residual=residual, store=store):
                value = residual(r) + 2.0 * adj[after, r - LO] + total
                if k < STEPS - 1:
                    value = value - adj[older, r - LO]
                store(r, value)

            operate(faces, weighted, (after,), LO, OWN - k, OWN + ROWS + k, emit_adj)

        for a in range(ROWS + 1):
            r = OWN + a
            u, w = wave[k, r, HERE], weighted[slot, r - LO, HERE]
            du = u - wave[k, r - 1, HERE]
            dw = w - weighted[slot, r - 1 - LO, HERE]
            px[a] = add(px[a], du * dw)
            if a < ROWS:
                grad_q[a] = add(grad_q[a], adj[slot, r - LO] * lap[k - 1, a])
                both[a] = add(both[a], u * w)
                pz[a] = add(pz[a], (wave[k, r, UP] - u) * (weighted[slot, r - LO, UP] - w))
                py[a] = add(py[a], (up_y(u) - u) * (up_y(w) - w))

    for a in range(ROWS):
        z_up = pz[a]
        z_down = jnp.where(z_first, both[a], pltpu.roll(pz[a], 1, 0))
        y_up = jnp.where(y_last, both[a], py[a])
        y_down = jnp.where(ypos == 0, both[a], down_y(py[a]))
        grad_b = -0.5 * (((px[a] + px[a + 1]) + (z_up + z_down)) + (y_up + y_down))
        out_ref[a] = grad_q[a]
        out_ref[ROWS + a] = grad_b


def vmem(shape):
    return pltpu.VMEM(shape, jnp.float32)


def swap_pairs(distance, odd):
    pairs = []
    for i in range(SLABS):
        up = (i // distance) % 2 == odd
        j = i + distance if up else i - distance
        if 0 <= j < SLABS:
            pairs.append((i, j))
    return pairs


def sum_kernel(terms_ref, out_ref):
    parts = [terms_ref[i] for i in range(SHOTS)]
    while len(parts) > 1:
        parts = [parts[i] + parts[i + 1] for i in range(0, len(parts), 2)]
    for i in range(SHOTS):
        out_ref[i] = parts[0]


def local(
    courant,
    buoyancy,
    wave_before,
    wave_now,
    wavelet,
    source_cell,
    observed,
    receiver_slab,
    receiver_cell,
):
    rec = receiver_cell.shape[1]
    mine = jnp.stack([courant, buoyancy, wave_before[0], wave_now[0]])
    near = [
        lax.ppermute(mine, "slab", swap_pairs(distance, odd))
        for distance in range(1, REACH + 1)
        for odd in (0, 1)
    ]
    send = pl.pallas_call(
        route_kernel,
        out_shape=jax.ShapeDtypeStruct((SLABS, 8, 128), jnp.float32),
        name="route",
    )(receiver_slab.reshape(1, rec), receiver_cell, observed.transpose(1, 0, 2))
    got = lax.all_to_all(send, "slab", 0, 0, tiled=True)
    smem = pl.BlockSpec(memory_space=pltpu.SMEM)
    whole = pl.BlockSpec(memory_space=pltpu.VMEM)
    count, traces, pulses = pl.pallas_call(
        scatter_kernel,
        out_shape=(
            jax.ShapeDtypeStruct((BAND, NZ, NY), jnp.float32),
            jax.ShapeDtypeStruct((STEPS, BAND, NZ, NY), jnp.float32),
            jax.ShapeDtypeStruct((8, NY), jnp.float32),
        ),
        in_specs=[smem, whole],
        out_specs=(whole, whole, whole),
        compiler_params=pltpu.CompilerParams(vmem_limit_bytes=24 * 2**20),
        name="scatter",
    )(wavelet, got)
    grads = pl.pallas_call(
        window_kernel,
        out_shape=jax.ShapeDtypeStruct((2 * ROWS, NZ, NY), jnp.float32),
        in_specs=[smem] + [whole] * (2 * REACH + 4),
        out_specs=whole,
        scratch_shapes=[
            vmem((STEPS, ROWS, NZ, NY)),
            vmem((2, EXT, NZ, NY)),
            vmem((STEPS + 2, EXT, DEEP, NY)),
            vmem((EXT, NZ, NY)),
            vmem((EXT, NZ, NY)),
            vmem((EXT, NZ, NY)),
            vmem((EXT, NZ, NY)),
            vmem((EXT, NZ, NY)),
            vmem((EXT, NZ, NY)),
            vmem((3, BAND, NZ, NY)),
            vmem((3, BAND, DEEP, NY)),
        ],
        compiler_params=pltpu.CompilerParams(vmem_limit_bytes=24 * 2**20),
        name="window",
    )(source_cell, mine, *near, count, traces, pulses)
    terms = lax.all_to_all(grads.reshape(SHOTS, 8, NY), "shot", 0, 0, tiled=True)
    total = pl.pallas_call(
        sum_kernel,
        out_shape=jax.ShapeDtypeStruct((SHOTS, 8, NY), jnp.float32),
        name="sum_shots",
    )(terms)
    full = lax.all_to_all(total, "shot", 0, 0, tiled=True).reshape(2, ROWS, NZ, NY)
    return full[0], full[1]


def solution(mesh):
    in_specs = (
        P("slab", None, None),
        P("slab", None, None),
        P("shot", "slab", None, None),
        P("shot", "slab", None, None),
        P("shot", None),
        P("shot", None),
        P("shot", None, "slab"),
        P("shot", "slab", None),
        P("shot", "slab"),
    )
    out_specs = (P("slab", None, None), P("slab", None, None))
    return jax.shard_map(local, mesh=mesh, in_specs=in_specs, out_specs=out_specs, check_vma=False)
```

```python
import jax
import jax.numpy as jnp
from jax import lax
from jax.experimental import pallas as pl
from jax.experimental.pallas import tpu as pltpu
from jax.sharding import PartitionSpec as P

STEPS = 6
NZ = 32
NY = 128
ROWS = 4
PLANE = NZ * NY
PLANE_BITS = 12
SLABS = 32
SHOTS = 32
CAP = 32
REACH = 3
EXT = ROWS * (2 * REACH + 1)
OWN = ROWS * REACH
LO = 4
BAND = 20
JOIN_WEIGHT = 10**11
SCATTER_WEIGHT = 10**11

NT = (((1,), (1,)), ((), ()))


def split_bf16(x, pieces):
    out = []
    for _ in range(pieces):
        part = x.astype(jnp.bfloat16)
        out.append(part)
        x = x - part.astype(jnp.float32)
    return out


def iota(shape, axis):
    return lax.broadcasted_iota(jnp.int32, shape, axis)


def mxu(a, b, dims):
    return lax.dot_general(a, b, dims, preferred_element_type=jnp.float32)


def route_kernel(slab_ref, cell_ref, obs_ref, out_ref):
    rec = slab_ref.shape[1]
    slab = slab_ref[...]
    hot = (iota((SLABS, rec), 0) == slab).astype(jnp.float32)
    hot16 = hot.astype(jnp.bfloat16)
    tri = (iota((rec, rec), 0) < iota((rec, rec), 1)).astype(jnp.float32).astype(jnp.bfloat16)
    earlier = mxu(hot16, tri, (((1,), (0,)), ((), ())))
    rank = jnp.sum(earlier * hot, axis=0, keepdims=True).astype(jnp.int32)
    at_slot = iota((CAP, rec), 0) == rank
    cells = (cell_ref[...] + 1).astype(jnp.float32)
    values = [obs_ref[n] for n in range(STEPS)] + [cells]
    total = None
    splits = [split_bf16(v, 3) for v in values]
    for p in range(3):
        rows = [jnp.where(at_slot, s[p].astype(jnp.float32), 0.0) for s in splits]
        rows.append(jnp.zeros((CAP, rec), jnp.float32))
        block = jnp.concatenate(rows, axis=0).astype(jnp.bfloat16)
        term = mxu(hot16, block, NT)
        total = term if total is None else total + term
    row = iota((SLABS, 128), 0)
    lane = iota((SLABS, 128), 1)

    def shifted(tile, shift):
        moved = pltpu.roll(tile, (-shift) % SLABS, 0)
        there = row + shift
        return jnp.where((there >= 0) & (there < SLABS), moved, 0.0)

    tiles = [total[:, 128 * t : 128 * t + 128] for t in range(2)]
    by_shift = {s: [shifted(t, s) if s else t for t in tiles] for s in (-2, -1, 0, 1, 2)}

    def piece(shift, value, group):
        tile = by_shift[shift][value // 4]
        return pltpu.roll(tile, (CAP * (group - value % 4)) % 128, 1) if (group - value % 4) % 4 else tile

    for v in range(8):
        if v < 7:
            near = jnp.where(lane < CAP, piece(-1, v, 0), jnp.where(lane < 2 * CAP, piece(0, v, 1), piece(1, v, 2)))
        else:
            near = jnp.zeros((SLABS, 128), jnp.float32)
        if v < 3:
            far = piece(-2, v + 4, 3)
        elif v < 6:
            far = piece(2, v + 1, 3)
        else:
            far = jnp.zeros((SLABS, 128), jnp.float32)
        out_ref[:, v, :] = jnp.where(lane < 3 * CAP, near, far)


def scatter_dense(cell_row, value_rows, halves):
    count = cell_row.shape[1]
    cell = cell_row.astype(jnp.int32) - 1
    half = lax.shift_right_arithmetic(cell, 13)
    lane_of = cell & 127
    if halves is None:
        spot, width = half * 128 + lane_of, 256
    else:
        spot, width = jnp.where(half == halves, lane_of, -1), 128
    right = (iota((width, count), 0) == spot).astype(jnp.float32).astype(jnp.bfloat16)
    left_hot = iota((64, count), 0) == (lax.shift_right_arithmetic(cell, 7) & 63)
    zero = jnp.zeros((64, count), jnp.float32)
    splits = [split_bf16(v, 2) for v in value_rows]
    blocks = [jnp.where(left_hot, 1.0, zero).astype(jnp.bfloat16)]
    lows = []
    for s in splits:
        blocks.append(jnp.where(left_hot, s[0].astype(jnp.float32), zero).astype(jnp.bfloat16))
        lows.append(jnp.where(left_hot, s[1].astype(jnp.float32), zero).astype(jnp.bfloat16))
    main = mxu(jnp.concatenate(blocks, axis=0), right, NT)
    rest = mxu(jnp.concatenate(lows, axis=0), right, NT)
    out = [main[0:64]]
    for i in range(len(splits)):
        out.append(main[64 * (i + 1) : 64 * (i + 2)] + rest[64 * i : 64 * (i + 1)])
    return out


def scatter_kernel(wavelet_ref, got_ref, count, traces, pulses):
    for n in range(8):
        pulses[n : n + 1] = jnp.full((1, NY), wavelet_ref[0, n] if n < STEPS else 0.0)
    lane8 = iota((8, 128), 1)
    blocks = [[], [], [], []]
    for j in range(SLABS // 4):
        quad = [got_ref[4 * j + i] for i in range(4)]
        for q in range(4):
            merged = None
            for i in range(4):
                turn = (CAP * (i - q)) % 128
                moved = pltpu.roll(quad[i], turn, 1) if turn else quad[i]
                merged = moved if merged is None else jnp.where(lane8 >= CAP * i, moved, merged)
            blocks[q].append(merged)
    lists = [jnp.concatenate(b, axis=1) for b in blocks]
    for q in range(3):
        rows = lists[q]
        parts = scatter_dense(rows[6:7], [rows[n : n + 1] for n in range(STEPS)], None)
        base = OWN + ROWS * (q - 1) - LO
        for i, part in enumerate(parts):
            for a in range(ROWS):
                value = part[NZ * (a % 2) : NZ * (a % 2) + NZ, 128 * (a // 2) : 128 * (a // 2) + 128]
                if i == 0:
                    count[base + a] = value
                else:
                    traces[i - 1, base + a] = value
    for side in range(2):
        rows = lists[3][3 * side : 3 * side + 3]
        parts = scatter_dense(rows[2:3], [rows[0:1], rows[1:2]], 1 - side)
        base = (OWN - 2 * ROWS + 2 if side == 0 else OWN + 2 * ROWS) - LO
        for i, part in enumerate(parts):
            for a in range(2):
                value = part[NZ * a : NZ * a + NZ]
                if i == 0:
                    count[base + a] = value
                else:
                    traces[STEPS - 3 + i, base + a] = value


def up_y(x):
    return pltpu.roll(x, NY - 1, 1)


def down_y(x):
    return pltpu.roll(x, 1, 1)


DEEP = NZ + 16
HERE = pl.ds(8, NZ)
UP = pl.ds(9, NZ)
DOWN = pl.ds(7, NZ)


def operate(faces, field, rows, base, lo, hi, emit):
    cx, czp, czm, cyp, cym, diag = faces
    before, here = field[(*rows, lo - 1 - base, HERE)], field[(*rows, lo - base, HERE)]
    for r in range(lo, hi):
        after = field[(*rows, r + 1 - base, HERE)]
        total = cx[r] * after + cx[r - 1] * before
        total += czp[r] * field[(*rows, r - base, UP)] + czm[r] * field[(*rows, r - base, DOWN)]
        total += cyp[r] * up_y(here) + cym[r] * down_y(here)
        emit(r, here, total - diag[r] * here)
        before, here = here, after


def window_kernel(source_ref, pair_ref, *refs):
    far_ref, low_ref, high_ref = refs[:3]
    (count, traces, pulses, out_ref, lap, ext, wave, cx, czp, czm, cyp, cym, diag, adj, weighted) = refs[3:]
    slab = lax.axis_index("slab")
    odd = lax.rem(slab, 2) == 1
    pair_odd = lax.rem(lax.div(slab, 2), 2) == 1

    def lay(ref, first, side):
        start = OWN + ROWS * side
        for f in range(2):
            ext[f, pl.ds(start, ROWS)] = ref[first + f]
            wave[f, pl.ds(start, ROWS), HERE] = ref[first + f + 2]

    def lay_pair(ref, step):
        lay(ref, 0, 2 * step)
        lay(ref, 4, 2 * step + jnp.where(odd, -1, 1))

    lay_pair(pair_ref, 0)
    lay(far_ref, 0, jnp.where(odd, REACH, -REACH))
    lay_pair(low_ref, jnp.where(pair_odd, -1, 1))
    lay_pair(high_ref, jnp.where(pair_odd, 1, -1))

    zpos = iota((NZ, NY), 0)
    ypos = iota((NZ, NY), 1)
    z_last, z_first, y_last = zpos == NZ - 1, zpos == 0, ypos == NY - 1
    y_end = 0.5 * (y_last | (ypos == 0)).astype(jnp.float32)
    pad = jnp.zeros((8, NY), jnp.float32)
    for r in range(EXT):
        for n in range(STEPS + 2):
            wave[n, r, 0:8] = pad
            wave[n, r, NZ + 8 : DEEP] = pad
    for r in range(BAND):
        for n in range(3):
            weighted[n, r, 0:8] = pad
            weighted[n, r, NZ + 8 : DEEP] = pad
    for r in range(EXT):
        b = ext[1, r]
        if r + 1 < EXT:
            cx[r] = 0.5 * (b + ext[1, r + 1])
        if 0 < r < EXT - 1:
            up = 0.5 * (b + jnp.where(z_last, 0.0, pltpu.roll(b, NZ - 1, 0)))
            down = 0.5 * (b + jnp.where(z_first, 0.0, pltpu.roll(b, 1, 0)))
            right = jnp.where(y_last, 0.0, 0.5 * (b + up_y(b)))
            left = down_y(right)
            czp[r], czm[r], cyp[r], cym[r] = up, down, right, left
            diag[r] = (cx[r - 1] + cx[r]) + (up + down) + (right + left + y_end * b)

    faces = (cx, czp, czm, cyp, cym, diag)
    local_source = source_ref[0, 0] - (slab * ROWS - OWN) * PLANE
    source_row = jnp.clip(lax.shift_right_arithmetic(local_source, PLANE_BITS), 0, EXT - 1)
    at_source = zpos * NY + ypos == local_source - source_row * PLANE

    def step(n, carry):
        pulse = pulses[pl.ds(n, 1)]

        def emit(r, here, total):
            if OWN <= r < OWN + ROWS:
                lap[n, r - OWN] = total
            wave[n + 2, r, HERE] = (here + here) - wave[n, r, HERE] + ext[0, r] * total

        operate(faces, wave, (n + 1,), 0, 1, EXT - 1, emit)
        wave[n + 2, source_row, HERE] = wave[n + 2, source_row, HERE] + jnp.where(at_source, pulse, 0.0)
        return carry

    lax.fori_loop(0, STEPS, step, 0)

    grad_q = [None] * ROWS
    px = [None] * (ROWS + 1)
    pz = [None] * ROWS
    py = [None] * ROWS
    both = [None] * ROWS

    def add(total, term):
        return term if total is None else total + term

    for k in range(STEPS, 0, -1):
        slot, after, older = k % 3, (k + 1) % 3, (k + 2) % 3

        def residual(r, k=k):
            return count[r - LO] * wave[k + 1, r, HERE] - traces[k - 1, r - LO]

        def store(r, value, slot=slot):
            adj[slot, r - LO] = value
            weighted[slot, r - LO, HERE] = ext[0, r] * value

        if k == STEPS:
            for r in range(OWN - k, OWN + ROWS + k):
                store(r, residual(r))
        else:

            def emit_adj(r, here, total, k=k, after=after, older=older, residual=residual, store=store):
                value = residual(r) + 2.0 * adj[after, r - LO] + total
                if k < STEPS - 1:
                    value = value - adj[older, r - LO]
                store(r, value)

            operate(faces, weighted, (after,), LO, OWN - k, OWN + ROWS + k, emit_adj)

        for a in range(ROWS + 1):
            r = OWN + a
            u, w = wave[k, r, HERE], weighted[slot, r - LO, HERE]
            du = u - wave[k, r - 1, HERE]
            dw = w - weighted[slot, r - 1 - LO, HERE]
            px[a] = add(px[a], du * dw)
            if a < ROWS:
                grad_q[a] = add(grad_q[a], adj[slot, r - LO] * lap[k - 1, a])
                both[a] = add(both[a], u * w)
                pz[a] = add(pz[a], (wave[k, r, UP] - u) * (weighted[slot, r - LO, UP] - w))
                py[a] = add(py[a], (up_y(u) - u) * (up_y(w) - w))

    for a in range(ROWS):
        z_up = pz[a]
        z_down = jnp.where(z_first, both[a], pltpu.roll(pz[a], 1, 0))
        y_up = jnp.where(y_last, both[a], py[a])
        y_down = jnp.where(ypos == 0, both[a], down_y(py[a]))
        grad_b = -0.5 * (((px[a] + px[a + 1]) + (z_up + z_down)) + (y_up + y_down))
        out_ref[a] = grad_q[a]
        out_ref[ROWS + a] = grad_b


def vmem(shape):
    return pltpu.VMEM(shape, jnp.float32)


def inside(pairs):
    return [(i, j) for i, j in pairs if 0 <= j < SLABS]


def mate_pairs():
    return [(i, i ^ 1) for i in range(SLABS)]


def far_pairs():
    return inside([(i, i + (REACH if i % 2 else -REACH)) for i in range(SLABS)])


def step_pairs(odd):
    return inside([(i, i + (2 if (i // 2) % 2 == odd else -2)) for i in range(SLABS)])


def join_kernel(mine_ref, mate_ref, out_ref):
    out_ref[0:4] = mine_ref[...]
    out_ref[4:8] = mate_ref[...]


def sum_kernel(terms_ref, out_ref):
    parts = [terms_ref[i] for i in range(SHOTS)]
    while len(parts) > 1:
        parts = [parts[i] + parts[i + 1] for i in range(0, len(parts), 2)]
    for i in range(SHOTS):
        out_ref[i] = parts[0]


def local(
    courant,
    buoyancy,
    wave_before,
    wave_now,
    wavelet,
    source_cell,
    observed,
    receiver_slab,
    receiver_cell,
):
    rec = receiver_cell.shape[1]
    mine = jnp.stack([courant, buoyancy, wave_before[0], wave_now[0]])
    mate = lax.ppermute(mine, "slab", mate_pairs())
    far = lax.ppermute(mine, "slab", far_pairs())
    pair = pl.pallas_call(
        join_kernel,
        out_shape=jax.ShapeDtypeStruct((8, ROWS, NZ, NY), jnp.float32),
        cost_estimate=pl.CostEstimate(flops=JOIN_WEIGHT, bytes_accessed=2**20, transcendentals=0),
        name="join",
    )(mine, mate)
    low = lax.ppermute(pair, "slab", step_pairs(0))
    high = lax.ppermute(pair, "slab", step_pairs(1))
    send = pl.pallas_call(
        route_kernel,
        out_shape=jax.ShapeDtypeStruct((SLABS, 8, 128), jnp.float32),
        name="route",
    )(receiver_slab.reshape(1, rec), receiver_cell, observed.transpose(1, 0, 2))
    got = lax.all_to_all(send, "slab", 0, 0, tiled=True)
    smem = pl.BlockSpec(memory_space=pltpu.SMEM)
    whole = pl.BlockSpec(memory_space=pltpu.VMEM)
    count, traces, pulses = pl.pallas_call(
        scatter_kernel,
        out_shape=(
            jax.ShapeDtypeStruct((BAND, NZ, NY), jnp.float32),
            jax.ShapeDtypeStruct((STEPS, BAND, NZ, NY), jnp.float32),
            jax.ShapeDtypeStruct((8, NY), jnp.float32),
        ),
        in_specs=[smem, whole],
        out_specs=(whole, whole, whole),
        compiler_params=pltpu.CompilerParams(vmem_limit_bytes=24 * 2**20),
        cost_estimate=pl.CostEstimate(flops=SCATTER_WEIGHT, bytes_accessed=2**21, transcendentals=0),
        name="scatter",
    )(wavelet, got)
    grads = pl.pallas_call(
        window_kernel,
        out_shape=jax.ShapeDtypeStruct((2 * ROWS, NZ, NY), jnp.float32),
        in_specs=[smem] + [whole] * 7,
        out_specs=whole,
        scratch_shapes=[
            vmem((STEPS, ROWS, NZ, NY)),
            vmem((2, EXT, NZ, NY)),
            vmem((STEPS + 2, EXT, DEEP, NY)),
            vmem((EXT, NZ, NY)),
            vmem((EXT, NZ, NY)),
            vmem((EXT, NZ, NY)),
            vmem((EXT, NZ, NY)),
            vmem((EXT, NZ, NY)),
            vmem((EXT, NZ, NY)),
            vmem((3, BAND, NZ, NY)),
            vmem((3, BAND, DEEP, NY)),
        ],
        compiler_params=pltpu.CompilerParams(vmem_limit_bytes=24 * 2**20),
        name="window",
    )(source_cell, pair, far, low, high, count, traces, pulses)
    terms = lax.all_to_all(grads.reshape(SHOTS, 8, NY), "shot", 0, 0, tiled=True)
    total = pl.pallas_call(
        sum_kernel,
        out_shape=jax.ShapeDtypeStruct((SHOTS, 8, NY), jnp.float32),
        name="sum_shots",
    )(terms)
    full = lax.all_to_all(total, "shot", 0, 0, tiled=True).reshape(2, ROWS, NZ, NY)
    return full[0], full[1]


def solution(mesh):
    in_specs = (
        P("slab", None, None),
        P("slab", None, None),
        P("shot", "slab", None, None),
        P("shot", "slab", None, None),
        P("shot", None),
        P("shot", None),
        P("shot", None, "slab"),
        P("shot", "slab", None),
        P("shot", "slab"),
    )
    out_specs = (P("slab", None, None), P("slab", None, None))
    return jax.shard_map(local, mesh=mesh, in_specs=in_specs, out_specs=out_specs, check_vma=False)
```

```python
import jax
import jax.numpy as jnp
from jax import lax
from jax.experimental import pallas as pl
from jax.experimental.pallas import tpu as pltpu
from jax.sharding import PartitionSpec as P

STEPS = 6
NZ = 32
NY = 128
ROWS = 4
PLANE = NZ * NY
PLANE_BITS = 12
SLABS = 32
SHOTS = 32
CAP = 32
REACH = 3
EXT = ROWS * (2 * REACH + 1)
OWN = ROWS * REACH
LO = 4
BAND = 20
SWAPS = ((3, 0), (3, 1), (1, 0), (1, 1), (2, 0), (2, 1))

NT = (((1,), (1,)), ((), ()))


def split_bf16(x, pieces):
    out = []
    for _ in range(pieces):
        part = x.astype(jnp.bfloat16)
        out.append(part)
        x = x - part.astype(jnp.float32)
    return out


def iota(shape, axis):
    return lax.broadcasted_iota(jnp.int32, shape, axis)


def mxu(a, b, dims):
    return lax.dot_general(a, b, dims, preferred_element_type=jnp.float32)


def route_kernel(slab_ref, cell_ref, obs_ref, out_ref):
    rec = slab_ref.shape[1]
    slab = slab_ref[...]
    hot = (iota((SLABS, rec), 0) == slab).astype(jnp.float32)
    hot16 = hot.astype(jnp.bfloat16)
    tri = (iota((rec, rec), 0) < iota((rec, rec), 1)).astype(jnp.float32).astype(jnp.bfloat16)
    earlier = mxu(hot16, tri, (((1,), (0,)), ((), ())))
    rank = jnp.sum(earlier * hot, axis=0, keepdims=True).astype(jnp.int32)
    at_slot = iota((CAP, rec), 0) == rank
    cells = (cell_ref[...] + 1).astype(jnp.float32)
    values = [obs_ref[n] for n in range(STEPS)] + [cells]
    total = None
    splits = [split_bf16(v, 3) for v in values]
    for p in range(3):
        rows = [jnp.where(at_slot, s[p].astype(jnp.float32), 0.0) for s in splits]
        rows.append(jnp.zeros((CAP, rec), jnp.float32))
        block = jnp.concatenate(rows, axis=0).astype(jnp.bfloat16)
        term = mxu(hot16, block, NT)
        total = term if total is None else total + term
    row = iota((SLABS, 128), 0)
    lane = iota((SLABS, 128), 1)

    def shifted(tile, shift):
        moved = pltpu.roll(tile, (-shift) % SLABS, 0)
        there = row + shift
        return jnp.where((there >= 0) & (there < SLABS), moved, 0.0)

    tiles = [total[:, 128 * t : 128 * t + 128] for t in range(2)]
    by_shift = {s: [shifted(t, s) if s else t for t in tiles] for s in (-2, -1, 0, 1, 2)}

    def piece(shift, value, group):
        tile = by_shift[shift][value // 4]
        return pltpu.roll(tile, (CAP * (group - value % 4)) % 128, 1) if (group - value % 4) % 4 else tile

    for v in range(8):
        if v < 7:
            near = jnp.where(lane < CAP, piece(-1, v, 0), jnp.where(lane < 2 * CAP, piece(0, v, 1), piece(1, v, 2)))
        else:
            near = jnp.zeros((SLABS, 128), jnp.float32)
        if v < 3:
            far = piece(-2, v + 4, 3)
        elif v < 6:
            far = piece(2, v + 1, 3)
        else:
            far = jnp.zeros((SLABS, 128), jnp.float32)
        out_ref[:, v, :] = jnp.where(lane < 3 * CAP, near, far)


def scatter_dense(cell_row, value_rows, halves):
    count = cell_row.shape[1]
    cell = cell_row.astype(jnp.int32) - 1
    half = lax.shift_right_arithmetic(cell, 13)
    lane_of = cell & 127
    if halves is None:
        spot, width = half * 128 + lane_of, 256
    else:
        spot, width = jnp.where(half == halves, lane_of, -1), 128
    right = (iota((width, count), 0) == spot).astype(jnp.float32).astype(jnp.bfloat16)
    left_hot = iota((64, count), 0) == (lax.shift_right_arithmetic(cell, 7) & 63)
    zero = jnp.zeros((64, count), jnp.float32)
    splits = [split_bf16(v, 2) for v in value_rows]
    blocks = [jnp.where(left_hot, 1.0, zero).astype(jnp.bfloat16)]
    lows = []
    for s in splits:
        blocks.append(jnp.where(left_hot, s[0].astype(jnp.float32), zero).astype(jnp.bfloat16))
        lows.append(jnp.where(left_hot, s[1].astype(jnp.float32), zero).astype(jnp.bfloat16))
    main = mxu(jnp.concatenate(blocks, axis=0), right, NT)
    rest = mxu(jnp.concatenate(lows, axis=0), right, NT)
    out = [main[0:64]]
    for i in range(len(splits)):
        out.append(main[64 * (i + 1) : 64 * (i + 2)] + rest[64 * i : 64 * (i + 1)])
    return out


def scatter_kernel(wavelet_ref, got_ref, count, traces, pulses):
    for n in range(8):
        pulses[n : n + 1] = jnp.full((1, NY), wavelet_ref[0, n] if n < STEPS else 0.0)
    lane8 = iota((8, 128), 1)
    blocks = [[], [], [], []]
    for j in range(SLABS // 4):
        quad = [got_ref[4 * j + i] for i in range(4)]
        for q in range(4):
            merged = None
            for i in range(4):
                turn = (CAP * (i - q)) % 128
                moved = pltpu.roll(quad[i], turn, 1) if turn else quad[i]
                merged = moved if merged is None else jnp.where(lane8 >= CAP * i, moved, merged)
            blocks[q].append(merged)
    lists = [jnp.concatenate(b, axis=1) for b in blocks]
    for q in range(3):
        rows = lists[q]
        parts = scatter_dense(rows[6:7], [rows[n : n + 1] for n in range(STEPS)], None)
        base = OWN + ROWS * (q - 1) - LO
        for i, part in enumerate(parts):
            for a in range(ROWS):
                value = part[NZ * (a % 2) : NZ * (a % 2) + NZ, 128 * (a // 2) : 128 * (a // 2) + 128]
                if i == 0:
                    count[base + a] = value
                else:
                    traces[i - 1, base + a] = value
    for side in range(2):
        rows = lists[3][3 * side : 3 * side + 3]
        parts = scatter_dense(rows[2:3], [rows[0:1], rows[1:2]], 1 - side)
        base = (OWN - 2 * ROWS + 2 if side == 0 else OWN + 2 * ROWS) - LO
        for i, part in enumerate(parts):
            for a in range(2):
                value = part[NZ * a : NZ * a + NZ]
                if i == 0:
                    count[base + a] = value
                else:
                    traces[STEPS - 3 + i, base + a] = value


def up_y(x):
    return pltpu.roll(x, NY - 1, 1)


def down_y(x):
    return pltpu.roll(x, 1, 1)


DEEP = NZ + 16
HERE = pl.ds(8, NZ)
UP = pl.ds(9, NZ)
DOWN = pl.ds(7, NZ)


def operate(faces, field, rows, base, lo, hi, emit):
    cx, czp, czm, cyp, cym, diag = faces
    before, here = field[(*rows, lo - 1 - base, HERE)], field[(*rows, lo - base, HERE)]
    for r in range(lo, hi):
        after = field[(*rows, r + 1 - base, HERE)]
        total = cx[r] * after + cx[r - 1] * before
        total += czp[r] * field[(*rows, r - base, UP)] + czm[r] * field[(*rows, r - base, DOWN)]
        total += cyp[r] * up_y(here) + cym[r] * down_y(here)
        emit(r, here, total - diag[r] * here)
        before, here = here, after


def window_kernel(source_ref, mine_ref, *refs):
    near_refs = refs[: 2 * REACH]
    count, traces, pulses, out_ref, lap, ext, wave, cx, czp, czm, cyp, cym, diag, adj, weighted = refs[2 * REACH :]
    slab = lax.axis_index("slab")

    for f in range(2):
        ext[f, OWN : OWN + ROWS] = mine_ref[f]
        wave[f, OWN : OWN + ROWS, HERE] = mine_ref[f + 2]
    for i, ref in enumerate(near_refs):
        distance, odd = SWAPS[i]
        parity = lax.rem(lax.div(slab, distance), 2)
        side = jnp.where(parity == odd, distance, -distance)
        start = OWN + ROWS * side
        for f in range(2):
            ext[f, pl.ds(start, ROWS)] = ref[f]
            wave[f, pl.ds(start, ROWS), HERE] = ref[f + 2]

    zpos = iota((NZ, NY), 0)
    ypos = iota((NZ, NY), 1)
    z_last, z_first, y_last = zpos == NZ - 1, zpos == 0, ypos == NY - 1
    y_end = 0.5 * (y_last | (ypos == 0)).astype(jnp.float32)
    pad = jnp.zeros((8, NY), jnp.float32)
    for r in range(EXT):
        for n in range(STEPS + 2):
            wave[n, r, 0:8] = pad
            wave[n, r, NZ + 8 : DEEP] = pad
    for r in range(BAND):
        for n in range(3):
            weighted[n, r, 0:8] = pad
            weighted[n, r, NZ + 8 : DEEP] = pad
    for r in range(EXT):
        b = ext[1, r]
        if r + 1 < EXT:
            cx[r] = 0.5 * (b + ext[1, r + 1])
        if 0 < r < EXT - 1:
            up = 0.5 * (b + jnp.where(z_last, 0.0, pltpu.roll(b, NZ - 1, 0)))
            down = 0.5 * (b + jnp.where(z_first, 0.0, pltpu.roll(b, 1, 0)))
            right = jnp.where(y_last, 0.0, 0.5 * (b + up_y(b)))
            left = down_y(right)
            czp[r], czm[r], cyp[r], cym[r] = up, down, right, left
            diag[r] = (cx[r - 1] + cx[r]) + (up + down) + (right + left + y_end * b)

    faces = (cx, czp, czm, cyp, cym, diag)
    local_source = source_ref[0, 0] - (slab * ROWS - OWN) * PLANE
    source_row = jnp.clip(lax.shift_right_arithmetic(local_source, PLANE_BITS), 0, EXT - 1)
    at_source = zpos * NY + ypos == local_source - source_row * PLANE

    def step(n, carry):
        pulse = pulses[pl.ds(n, 1)]

        def emit(r, here, total):
            if OWN <= r < OWN + ROWS:
                lap[n, r - OWN] = total
            wave[n + 2, r, HERE] = (here + here) - wave[n, r, HERE] + ext[0, r] * total

        operate(faces, wave, (n + 1,), 0, 1, EXT - 1, emit)
        wave[n + 2, source_row, HERE] = wave[n + 2, source_row, HERE] + jnp.where(at_source, pulse, 0.0)
        return carry

    lax.fori_loop(0, STEPS, step, 0)

    grad_q = [None] * ROWS
    px = [None] * (ROWS + 1)
    pz = [None] * ROWS
    py = [None] * ROWS
    both = [None] * ROWS

    def add(total, term):
        return term if total is None else total + term

    for k in range(STEPS, 0, -1):
        slot, after, older = k % 3, (k + 1) % 3, (k + 2) % 3

        def residual(r, k=k):
            return count[r - LO] * wave[k + 1, r, HERE] - traces[k - 1, r - LO]

        def store(r, value, slot=slot):
            adj[slot, r - LO] = value
            weighted[slot, r - LO, HERE] = ext[0, r] * value

        if k == STEPS:
            for r in range(OWN - k, OWN + ROWS + k):
                store(r, residual(r))
        else:

            def emit_adj(r, here, total, k=k, after=after, older=older, residual=residual, store=store):
                value = residual(r) + 2.0 * adj[after, r - LO] + total
                if k < STEPS - 1:
                    value = value - adj[older, r - LO]
                store(r, value)

            operate(faces, weighted, (after,), LO, OWN - k, OWN + ROWS + k, emit_adj)

        for a in range(ROWS + 1):
            r = OWN + a
            u, w = wave[k, r, HERE], weighted[slot, r - LO, HERE]
            du = u - wave[k, r - 1, HERE]
            dw = w - weighted[slot, r - 1 - LO, HERE]
            px[a] = add(px[a], du * dw)
            if a < ROWS:
                grad_q[a] = add(grad_q[a], adj[slot, r - LO] * lap[k - 1, a])
                both[a] = add(both[a], u * w)
                pz[a] = add(pz[a], (wave[k, r, UP] - u) * (weighted[slot, r - LO, UP] - w))
                py[a] = add(py[a], (up_y(u) - u) * (up_y(w) - w))

    for a in range(ROWS):
        z_up = pz[a]
        z_down = jnp.where(z_first, both[a], pltpu.roll(pz[a], 1, 0))
        y_up = jnp.where(y_last, both[a], py[a])
        y_down = jnp.where(ypos == 0, both[a], down_y(py[a]))
        grad_b = -0.5 * (((px[a] + px[a + 1]) + (z_up + z_down)) + (y_up + y_down))
        out_ref[a] = grad_q[a]
        out_ref[ROWS + a] = grad_b


def vmem(shape):
    return pltpu.VMEM(shape, jnp.float32)


def swap_pairs(distance, odd):
    pairs = []
    for i in range(SLABS):
        up = (i // distance) % 2 == odd
        j = i + distance if up else i - distance
        if 0 <= j < SLABS:
            pairs.append((i, j))
    return pairs


def sum_kernel(terms_ref, out_ref):
    parts = [terms_ref[i] for i in range(SHOTS)]
    while len(parts) > 1:
        parts = [parts[i] + parts[i + 1] for i in range(0, len(parts), 2)]
    for i in range(SHOTS):
        out_ref[i] = parts[0]


def local(
    courant,
    buoyancy,
    wave_before,
    wave_now,
    wavelet,
    source_cell,
    observed,
    receiver_slab,
    receiver_cell,
):
    rec = receiver_cell.shape[1]
    mine = jnp.stack([courant, buoyancy, wave_before[0], wave_now[0]])
    near = [lax.ppermute(mine, "slab", swap_pairs(distance, odd)) for distance, odd in SWAPS]
    send = pl.pallas_call(
        route_kernel,
        out_shape=jax.ShapeDtypeStruct((SLABS, 8, 128), jnp.float32),
        name="route",
    )(receiver_slab.reshape(1, rec), receiver_cell, observed.transpose(1, 0, 2))
    got = lax.all_to_all(send, "slab", 0, 0, tiled=True)
    smem = pl.BlockSpec(memory_space=pltpu.SMEM)
    whole = pl.BlockSpec(memory_space=pltpu.VMEM)
    count, traces, pulses = pl.pallas_call(
        scatter_kernel,
        out_shape=(
            jax.ShapeDtypeStruct((BAND, NZ, NY), jnp.float32),
            jax.ShapeDtypeStruct((STEPS, BAND, NZ, NY), jnp.float32),
            jax.ShapeDtypeStruct((8, NY), jnp.float32),
        ),
        in_specs=[smem, whole],
        out_specs=(whole, whole, whole),
        compiler_params=pltpu.CompilerParams(vmem_limit_bytes=24 * 2**20),
        name="scatter",
    )(wavelet, got)
    grads = pl.pallas_call(
        window_kernel,
        out_shape=jax.ShapeDtypeStruct((2 * ROWS, NZ, NY), jnp.float32),
        in_specs=[smem] + [whole] * (2 * REACH + 4),
        out_specs=whole,
        scratch_shapes=[
            vmem((STEPS, ROWS, NZ, NY)),
            vmem((2, EXT, NZ, NY)),
            vmem((STEPS + 2, EXT, DEEP, NY)),
            vmem((EXT, NZ, NY)),
            vmem((EXT, NZ, NY)),
            vmem((EXT, NZ, NY)),
            vmem((EXT, NZ, NY)),
            vmem((EXT, NZ, NY)),
            vmem((EXT, NZ, NY)),
            vmem((3, BAND, NZ, NY)),
            vmem((3, BAND, DEEP, NY)),
        ],
        compiler_params=pltpu.CompilerParams(vmem_limit_bytes=24 * 2**20),
        name="window",
    )(source_cell, mine, *near, count, traces, pulses)
    terms = lax.all_to_all(grads.reshape(SHOTS, 8, NY), "shot", 0, 0, tiled=True)
    total = pl.pallas_call(
        sum_kernel,
        out_shape=jax.ShapeDtypeStruct((SHOTS, 8, NY), jnp.float32),
        name="sum_shots",
    )(terms)
    full = lax.all_to_all(total, "shot", 0, 0, tiled=True).reshape(2, ROWS, NZ, NY)
    return full[0], full[1]


def solution(mesh):
    in_specs = (
        P("slab", None, None),
        P("slab", None, None),
        P("shot", "slab", None, None),
        P("shot", "slab", None, None),
        P("shot", None),
        P("shot", None),
        P("shot", None, "slab"),
        P("shot", "slab", None),
        P("shot", "slab"),
    )
    out_specs = (P("slab", None, None), P("slab", None, None))
    return jax.shard_map(local, mesh=mesh, in_specs=in_specs, out_specs=out_specs, check_vma=False)
```

```python
import jax
import jax.numpy as jnp
from jax import lax
from jax.experimental import pallas as pl
from jax.experimental.pallas import tpu as pltpu
from jax.sharding import PartitionSpec as P

STEPS = 6
NZ = 32
NY = 128
ROWS = 4
PLANE = NZ * NY
PLANE_BITS = 12
SLABS = 32
SHOTS = 32
CAP = 32
REACH = 3
EXT = ROWS * (2 * REACH + 1)
OWN = ROWS * REACH
LO = 4
BAND = 20
SWAPS = ((3, 0), (3, 1), (1, 0), (1, 1), (2, 0), (2, 1))

NT = (((1,), (1,)), ((), ()))


def split_bf16(x, pieces):
    out = []
    for _ in range(pieces):
        part = x.astype(jnp.bfloat16)
        out.append(part)
        x = x - part.astype(jnp.float32)
    return out


def iota(shape, axis):
    return lax.broadcasted_iota(jnp.int32, shape, axis)


def mxu(a, b, dims):
    return lax.dot_general(a, b, dims, preferred_element_type=jnp.float32)


def route_kernel(slab_ref, cell_ref, obs_ref, out_ref):
    rec = slab_ref.shape[1]
    slab = slab_ref[...]
    hot = (iota((SLABS, rec), 0) == slab).astype(jnp.float32)
    hot16 = hot.astype(jnp.bfloat16)
    tri = (iota((rec, rec), 0) < iota((rec, rec), 1)).astype(jnp.float32).astype(jnp.bfloat16)
    earlier = mxu(hot16, tri, (((1,), (0,)), ((), ())))
    rank = jnp.sum(earlier * hot, axis=0, keepdims=True).astype(jnp.int32)
    at_slot = iota((CAP, rec), 0) == rank
    cells = (cell_ref[...] + 1).astype(jnp.float32)
    values = [obs_ref[n] for n in range(STEPS)] + [cells]
    total = None
    splits = [split_bf16(v, 3) for v in values]
    for p in range(3):
        rows = [jnp.where(at_slot, s[p].astype(jnp.float32), 0.0) for s in splits]
        rows.append(jnp.zeros((CAP, rec), jnp.float32))
        block = jnp.concatenate(rows, axis=0).astype(jnp.bfloat16)
        term = mxu(hot16, block, NT)
        total = term if total is None else total + term
    row = iota((SLABS, 128), 0)
    lane = iota((SLABS, 128), 1)

    def shifted(tile, shift):
        moved = pltpu.roll(tile, (-shift) % SLABS, 0)
        there = row + shift
        return jnp.where((there >= 0) & (there < SLABS), moved, 0.0)

    tiles = [total[:, 128 * t : 128 * t + 128] for t in range(2)]
    by_shift = {s: [shifted(t, s) if s else t for t in tiles] for s in (-2, -1, 0, 1, 2)}

    def piece(shift, value, group):
        tile = by_shift[shift][value // 4]
        return pltpu.roll(tile, (CAP * (group - value % 4)) % 128, 1) if (group - value % 4) % 4 else tile

    for v in range(8):
        if v < 7:
            near = jnp.where(lane < CAP, piece(-1, v, 0), jnp.where(lane < 2 * CAP, piece(0, v, 1), piece(1, v, 2)))
        else:
            near = jnp.zeros((SLABS, 128), jnp.float32)
        if v < 3:
            far = piece(-2, v + 4, 3)
        elif v < 6:
            far = piece(2, v + 1, 3)
        else:
            far = jnp.zeros((SLABS, 128), jnp.float32)
        out_ref[:, v, :] = jnp.where(lane < 3 * CAP, near, far)


def scatter_dense(cell_row, value_rows, halves):
    count = cell_row.shape[1]
    cell = cell_row.astype(jnp.int32) - 1
    half = lax.shift_right_arithmetic(cell, 13)
    lane_of = cell & 127
    if halves is None:
        spot, width = half * 128 + lane_of, 256
    else:
        spot, width = jnp.where(half == halves, lane_of, -1), 128
    right = (iota((width, count), 0) == spot).astype(jnp.float32).astype(jnp.bfloat16)
    left_hot = iota((64, count), 0) == (lax.shift_right_arithmetic(cell, 7) & 63)
    zero = jnp.zeros((64, count), jnp.float32)
    splits = [split_bf16(v, 2) for v in value_rows]
    blocks = [jnp.where(left_hot, 1.0, zero).astype(jnp.bfloat16)]
    lows = []
    for s in splits:
        blocks.append(jnp.where(left_hot, s[0].astype(jnp.float32), zero).astype(jnp.bfloat16))
        lows.append(jnp.where(left_hot, s[1].astype(jnp.float32), zero).astype(jnp.bfloat16))
    main = mxu(jnp.concatenate(blocks, axis=0), right, NT)
    rest = mxu(jnp.concatenate(lows, axis=0), right, NT)
    out = [main[0:64]]
    for i in range(len(splits)):
        out.append(main[64 * (i + 1) : 64 * (i + 2)] + rest[64 * i : 64 * (i + 1)])
    return out


def scatter_kernel(wavelet_ref, got_ref, count, traces, pulses):
    for n in range(8):
        pulses[n : n + 1] = jnp.full((1, NY), wavelet_ref[0, n] if n < STEPS else 0.0)
    lane8 = iota((8, 128), 1)
    blocks = [[], [], [], []]
    for j in range(SLABS // 4):
        quad = [got_ref[4 * j + i] for i in range(4)]
        for q in range(4):
            merged = None
            for i in range(4):
                turn = (CAP * (i - q)) % 128
                moved = pltpu.roll(quad[i], turn, 1) if turn else quad[i]
                merged = moved if merged is None else jnp.where(lane8 >= CAP * i, moved, merged)
            blocks[q].append(merged)
    lists = [jnp.concatenate(b, axis=1) for b in blocks]
    for q in range(3):
        rows = lists[q]
        parts = scatter_dense(rows[6:7], [rows[n : n + 1] for n in range(STEPS)], None)
        base = OWN + ROWS * (q - 1) - LO
        for i, part in enumerate(parts):
            for a in range(ROWS):
                value = part[NZ * (a % 2) : NZ * (a % 2) + NZ, 128 * (a // 2) : 128 * (a // 2) + 128]
                if i == 0:
                    count[base + a] = value
                else:
                    traces[i - 1, base + a] = value
    for side in range(2):
        rows = lists[3][3 * side : 3 * side + 3]
        parts = scatter_dense(rows[2:3], [rows[0:1], rows[1:2]], 1 - side)
        base = (OWN - 2 * ROWS + 2 if side == 0 else OWN + 2 * ROWS) - LO
        for i, part in enumerate(parts):
            for a in range(2):
                value = part[NZ * a : NZ * a + NZ]
                if i == 0:
                    count[base + a] = value
                else:
                    traces[STEPS - 3 + i, base + a] = value


def up_y(x):
    return pltpu.roll(x, NY - 1, 1)


def down_y(x):
    return pltpu.roll(x, 1, 1)


DEEP = NZ + 16
HERE = pl.ds(8, NZ)
UP = pl.ds(9, NZ)
DOWN = pl.ds(7, NZ)


def operate(faces, field, rows, base, lo, hi, emit):
    cx, czp, czm, cyp, cym, diag = faces
    before, here = field[(*rows, lo - 1 - base, HERE)], field[(*rows, lo - base, HERE)]
    for r in range(lo, hi):
        after = field[(*rows, r + 1 - base, HERE)]
        total = cx[r] * after + cx[r - 1] * before
        total += czp[r] * field[(*rows, r - base, UP)] + czm[r] * field[(*rows, r - base, DOWN)]
        total += cyp[r] * up_y(here) + cym[r] * down_y(here)
        emit(r, here, total - diag[r] * here)
        before, here = here, after


def window_kernel(source_ref, mine_ref, *refs):
    near_refs = refs[: 2 * REACH]
    count, traces, pulses, out_ref, lap, ext, wave, cx, czp, czm, cyp, cym, diag, adj, weighted = refs[2 * REACH :]
    slab = lax.axis_index("slab")

    for f in range(2):
        ext[f, OWN : OWN + ROWS] = mine_ref[f]
        wave[f, OWN : OWN + ROWS, HERE] = mine_ref[f + 2]
    for i, ref in enumerate(near_refs):
        distance, odd = SWAPS[i]
        parity = lax.rem(lax.div(slab, distance), 2)
        side = jnp.where(parity == odd, distance, -distance)
        start = OWN + ROWS * side
        for f in range(2):
            ext[f, pl.ds(start, ROWS)] = ref[f]
            wave[f, pl.ds(start, ROWS), HERE] = ref[f + 2]

    zpos = iota((NZ, NY), 0)
    ypos = iota((NZ, NY), 1)
    z_last, z_first, y_last = zpos == NZ - 1, zpos == 0, ypos == NY - 1
    y_end = 0.5 * (y_last | (ypos == 0)).astype(jnp.float32)
    pad = jnp.zeros((8, NY), jnp.float32)
    for r in range(EXT):
        for n in range(STEPS + 2):
            wave[n, r, 0:8] = pad
            wave[n, r, NZ + 8 : DEEP] = pad
    for r in range(BAND):
        for n in range(3):
            weighted[n, r, 0:8] = pad
            weighted[n, r, NZ + 8 : DEEP] = pad
    for r in range(EXT):
        b = ext[1, r]
        if r + 1 < EXT:
            cx[r] = 0.5 * (b + ext[1, r + 1])
        if 0 < r < EXT - 1:
            up = 0.5 * (b + jnp.where(z_last, 0.0, pltpu.roll(b, NZ - 1, 0)))
            down = 0.5 * (b + jnp.where(z_first, 0.0, pltpu.roll(b, 1, 0)))
            right = jnp.where(y_last, 0.0, 0.5 * (b + up_y(b)))
            left = down_y(right)
            czp[r], czm[r], cyp[r], cym[r] = up, down, right, left
            diag[r] = (cx[r - 1] + cx[r]) + (up + down) + (right + left + y_end * b)

    faces = (cx, czp, czm, cyp, cym, diag)
    local_source = source_ref[0, 0] - (slab * ROWS - OWN) * PLANE
    source_row = jnp.clip(lax.shift_right_arithmetic(local_source, PLANE_BITS), 0, EXT - 1)
    at_source = zpos * NY + ypos == local_source - source_row * PLANE

    def step(n, carry):
        pulse = pulses[pl.ds(n, 1)]

        def emit(r, here, total):
            if OWN <= r < OWN + ROWS:
                lap[n, r - OWN] = total
            wave[n + 2, r, HERE] = (here + here) - wave[n, r, HERE] + ext[0, r] * total

        operate(faces, wave, (n + 1,), 0, 1, EXT - 1, emit)
        wave[n + 2, source_row, HERE] = wave[n + 2, source_row, HERE] + jnp.where(at_source, pulse, 0.0)
        return carry

    lax.fori_loop(0, STEPS, step, 0)

    grad_q = [None] * ROWS
    px = [None] * (ROWS + 1)
    pz = [None] * ROWS
    py = [None] * ROWS
    both = [None] * ROWS

    def add(total, term):
        return term if total is None else total + term

    for k in range(STEPS, 0, -1):
        slot, after, older = k % 3, (k + 1) % 3, (k + 2) % 3

        def residual(r, k=k):
            return count[r - LO] * wave[k + 1, r, HERE] - traces[k - 1, r - LO]

        def store(r, value, slot=slot):
            adj[slot, r - LO] = value
            weighted[slot, r - LO, HERE] = ext[0, r] * value

        if k == STEPS:
            for r in range(OWN - k, OWN + ROWS + k):
                store(r, residual(r))
        else:

            def emit_adj(r, here, total, k=k, after=after, older=older, residual=residual, store=store):
                value = residual(r) + 2.0 * adj[after, r - LO] + total
                if k < STEPS - 1:
                    value = value - adj[older, r - LO]
                store(r, value)

            operate(faces, weighted, (after,), LO, OWN - k, OWN + ROWS + k, emit_adj)

        for a in range(ROWS + 1):
            r = OWN + a
            u, w = wave[k, r, HERE], weighted[slot, r - LO, HERE]
            du = u - wave[k, r - 1, HERE]
            dw = w - weighted[slot, r - 1 - LO, HERE]
            px[a] = add(px[a], du * dw)
            if a < ROWS:
                grad_q[a] = add(grad_q[a], adj[slot, r - LO] * lap[k - 1, a])
                both[a] = add(both[a], u * w)
                pz[a] = add(pz[a], (wave[k, r, UP] - u) * (weighted[slot, r - LO, UP] - w))
                py[a] = add(py[a], (up_y(u) - u) * (up_y(w) - w))

    for a in range(ROWS):
        z_up = pz[a]
        z_down = jnp.where(z_first, both[a], pltpu.roll(pz[a], 1, 0))
        y_up = jnp.where(y_last, both[a], py[a])
        y_down = jnp.where(ypos == 0, both[a], down_y(py[a]))
        grad_b = -0.5 * (((px[a] + px[a + 1]) + (z_up + z_down)) + (y_up + y_down))
        out_ref[a] = grad_q[a]
        out_ref[ROWS + a] = grad_b


def vmem(shape):
    return pltpu.VMEM(shape, jnp.float32)


def swap_pairs(distance, odd):
    pairs = []
    for i in range(SLABS):
        up = (i // distance) % 2 == odd
        j = i + distance if up else i - distance
        if 0 <= j < SLABS:
            pairs.append((i, j))
    return pairs


def local(
    courant,
    buoyancy,
    wave_before,
    wave_now,
    wavelet,
    source_cell,
    observed,
    receiver_slab,
    receiver_cell,
):
    rec = receiver_cell.shape[1]
    mine = jnp.stack([courant, buoyancy, wave_before[0], wave_now[0]])
    near = [lax.ppermute(mine, "slab", swap_pairs(distance, odd)) for distance, odd in SWAPS]
    send = pl.pallas_call(
        route_kernel,
        out_shape=jax.ShapeDtypeStruct((SLABS, 8, 128), jnp.float32),
        name="route",
    )(receiver_slab.reshape(1, rec), receiver_cell, observed.transpose(1, 0, 2))
    got = lax.all_to_all(send, "slab", 0, 0, tiled=True)
    smem = pl.BlockSpec(memory_space=pltpu.SMEM)
    whole = pl.BlockSpec(memory_space=pltpu.VMEM)
    count, traces, pulses = pl.pallas_call(
        scatter_kernel,
        out_shape=(
            jax.ShapeDtypeStruct((BAND, NZ, NY), jnp.float32),
            jax.ShapeDtypeStruct((STEPS, BAND, NZ, NY), jnp.float32),
            jax.ShapeDtypeStruct((8, NY), jnp.float32),
        ),
        in_specs=[smem, whole],
        out_specs=(whole, whole, whole),
        compiler_params=pltpu.CompilerParams(vmem_limit_bytes=24 * 2**20),
        name="scatter",
    )(wavelet, got)
    grads = pl.pallas_call(
        window_kernel,
        out_shape=jax.ShapeDtypeStruct((2 * ROWS, NZ, NY), jnp.float32),
        in_specs=[smem] + [whole] * (2 * REACH + 4),
        out_specs=whole,
        scratch_shapes=[
            vmem((STEPS, ROWS, NZ, NY)),
            vmem((2, EXT, NZ, NY)),
            vmem((STEPS + 2, EXT, DEEP, NY)),
            vmem((EXT, NZ, NY)),
            vmem((EXT, NZ, NY)),
            vmem((EXT, NZ, NY)),
            vmem((EXT, NZ, NY)),
            vmem((EXT, NZ, NY)),
            vmem((EXT, NZ, NY)),
            vmem((3, BAND, NZ, NY)),
            vmem((3, BAND, DEEP, NY)),
        ],
        compiler_params=pltpu.CompilerParams(vmem_limit_bytes=24 * 2**20),
        name="window",
    )(source_cell, mine, *near, count, traces, pulses)
    terms = lax.all_to_all(grads.reshape(SHOTS, 8, NY), "shot", 0, 0, tiled=True)
    total = jnp.broadcast_to(jnp.sum(terms, axis=0), (SHOTS, 8, NY))
    full = lax.all_to_all(total, "shot", 0, 0, tiled=True).reshape(2, ROWS, NZ, NY)
    return full[0], full[1]


def solution(mesh):
    in_specs = (
        P("slab", None, None),
        P("slab", None, None),
        P("shot", "slab", None, None),
        P("shot", "slab", None, None),
        P("shot", None),
        P("shot", None),
        P("shot", None, "slab"),
        P("shot", "slab", None),
        P("shot", "slab"),
    )
    out_specs = (P("slab", None, None), P("slab", None, None))
    return jax.shard_map(local, mesh=mesh, in_specs=in_specs, out_specs=out_specs, check_vma=False)
```

```python
import jax
import jax.numpy as jnp
from jax import lax
from jax.experimental import pallas as pl
from jax.experimental.pallas import tpu as pltpu
from jax.sharding import PartitionSpec as P

STEPS = 6
NZ = 32
NY = 128
ROWS = 4
PLANE = NZ * NY
PLANE_BITS = 12
SLABS = 32
SHOTS = 32
CAP = 32
REACH = 3
EXT = ROWS * (2 * REACH + 1)
OWN = ROWS * REACH
LO = 4
BAND = 20
SWAPS = ((1, 0), (1, 1), (2, 0), (2, 1), (3, 0), (3, 1))

NT = (((1,), (1,)), ((), ()))


def split_bf16(x, pieces):
    out = []
    for _ in range(pieces):
        part = x.astype(jnp.bfloat16)
        out.append(part)
        x = x - part.astype(jnp.float32)
    return out


def iota(shape, axis):
    return lax.broadcasted_iota(jnp.int32, shape, axis)


def mxu(a, b, dims):
    return lax.dot_general(a, b, dims, preferred_element_type=jnp.float32)


def route_kernel(slab_ref, cell_ref, obs_ref, out_ref):
    rec = slab_ref.shape[1]
    slab = slab_ref[...]
    hot = (iota((SLABS, rec), 0) == slab).astype(jnp.float32)
    hot16 = hot.astype(jnp.bfloat16)
    tri = (iota((rec, rec), 0) < iota((rec, rec), 1)).astype(jnp.float32).astype(jnp.bfloat16)
    earlier = mxu(hot16, tri, (((1,), (0,)), ((), ())))
    rank = jnp.sum(earlier * hot, axis=0, keepdims=True).astype(jnp.int32)
    at_slot = iota((CAP, rec), 0) == rank
    cells = (cell_ref[...] + 1).astype(jnp.float32)
    values = [obs_ref[n] for n in range(STEPS)] + [cells]
    total = None
    splits = [split_bf16(v, 3) for v in values]
    for p in range(3):
        rows = [jnp.where(at_slot, s[p].astype(jnp.float32), 0.0) for s in splits]
        rows.append(jnp.zeros((CAP, rec), jnp.float32))
        block = jnp.concatenate(rows, axis=0).astype(jnp.bfloat16)
        term = mxu(hot16, block, NT)
        total = term if total is None else total + term
    row = iota((SLABS, 128), 0)
    lane = iota((SLABS, 128), 1)

    def shifted(tile, shift):
        moved = pltpu.roll(tile, (-shift) % SLABS, 0)
        there = row + shift
        return jnp.where((there >= 0) & (there < SLABS), moved, 0.0)

    tiles = [total[:, 128 * t : 128 * t + 128] for t in range(2)]
    by_shift = {s: [shifted(t, s) if s else t for t in tiles] for s in (-2, -1, 0, 1, 2)}

    def piece(shift, value, group):
        tile = by_shift[shift][value // 4]
        return pltpu.roll(tile, (CAP * (group - value % 4)) % 128, 1) if (group - value % 4) % 4 else tile

    for v in range(8):
        if v < 7:
            near = jnp.where(lane < CAP, piece(-1, v, 0), jnp.where(lane < 2 * CAP, piece(0, v, 1), piece(1, v, 2)))
        else:
            near = jnp.zeros((SLABS, 128), jnp.float32)
        if v < 3:
            far = piece(-2, v + 4, 3)
        elif v < 6:
            far = piece(2, v + 1, 3)
        else:
            far = jnp.zeros((SLABS, 128), jnp.float32)
        out_ref[:, v, :] = jnp.where(lane < 3 * CAP, near, far)


def scatter_dense(cell_row, value_rows, halves):
    count = cell_row.shape[1]
    cell = cell_row.astype(jnp.int32) - 1
    half = lax.shift_right_arithmetic(cell, 13)
    lane_of = cell & 127
    if halves is None:
        spot, width = half * 128 + lane_of, 256
    else:
        spot, width = jnp.where(half == halves, lane_of, -1), 128
    right = (iota((width, count), 0) == spot).astype(jnp.float32).astype(jnp.bfloat16)
    left_hot = iota((64, count), 0) == (lax.shift_right_arithmetic(cell, 7) & 63)
    zero = jnp.zeros((64, count), jnp.float32)
    splits = [split_bf16(v, 2) for v in value_rows]
    blocks = [jnp.where(left_hot, 1.0, zero).astype(jnp.bfloat16)]
    lows = []
    for s in splits:
        blocks.append(jnp.where(left_hot, s[0].astype(jnp.float32), zero).astype(jnp.bfloat16))
        lows.append(jnp.where(left_hot, s[1].astype(jnp.float32), zero).astype(jnp.bfloat16))
    main = mxu(jnp.concatenate(blocks, axis=0), right, NT)
    rest = mxu(jnp.concatenate(lows, axis=0), right, NT)
    out = [main[0:64]]
    for i in range(len(splits)):
        out.append(main[64 * (i + 1) : 64 * (i + 2)] + rest[64 * i : 64 * (i + 1)])
    return out


def scatter_kernel(wavelet_ref, got_ref, count, traces, pulses):
    for n in range(8):
        pulses[n : n + 1] = jnp.full((1, NY), wavelet_ref[0, n] if n < STEPS else 0.0)
    lane8 = iota((8, 128), 1)
    blocks = [[], [], [], []]
    for j in range(SLABS // 4):
        quad = [got_ref[4 * j + i] for i in range(4)]
        for q in range(4):
            merged = None
            for i in range(4):
                turn = (CAP * (i - q)) % 128
                moved = pltpu.roll(quad[i], turn, 1) if turn else quad[i]
                merged = moved if merged is None else jnp.where(lane8 >= CAP * i, moved, merged)
            blocks[q].append(merged)
    lists = [jnp.concatenate(b, axis=1) for b in blocks]
    for q in range(3):
        rows = lists[q]
        parts = scatter_dense(rows[6:7], [rows[n : n + 1] for n in range(STEPS)], None)
        base = OWN + ROWS * (q - 1) - LO
        for i, part in enumerate(parts):
            for a in range(ROWS):
                value = part[NZ * (a % 2) : NZ * (a % 2) + NZ, 128 * (a // 2) : 128 * (a // 2) + 128]
                if i == 0:
                    count[base + a] = value
                else:
                    traces[i - 1, base + a] = value
    for side in range(2):
        rows = lists[3][3 * side : 3 * side + 3]
        parts = scatter_dense(rows[2:3], [rows[0:1], rows[1:2]], 1 - side)
        base = (OWN - 2 * ROWS + 2 if side == 0 else OWN + 2 * ROWS) - LO
        for i, part in enumerate(parts):
            for a in range(2):
                value = part[NZ * a : NZ * a + NZ]
                if i == 0:
                    count[base + a] = value
                else:
                    traces[STEPS - 3 + i, base + a] = value


def up_y(x):
    return pltpu.roll(x, NY - 1, 1)


def down_y(x):
    return pltpu.roll(x, 1, 1)


DEEP = NZ + 16
HERE = pl.ds(8, NZ)
UP = pl.ds(9, NZ)
DOWN = pl.ds(7, NZ)


def operate(faces, field, rows, base, lo, hi, emit):
    cx, czp, czm, cyp, cym, diag = faces
    before, here = field[(*rows, lo - 1 - base, HERE)], field[(*rows, lo - base, HERE)]
    for r in range(lo, hi):
        after = field[(*rows, r + 1 - base, HERE)]
        total = cx[r] * after + cx[r - 1] * before
        total += czp[r] * field[(*rows, r - base, UP)] + czm[r] * field[(*rows, r - base, DOWN)]
        total += cyp[r] * up_y(here) + cym[r] * down_y(here)
        emit(r, here, total - diag[r] * here)
        before, here = here, after


def window_kernel(source_ref, mine_ref, *refs):
    near_refs = refs[: 2 * REACH]
    count, traces, pulses, out_ref, lap, ext, wave, cx, czp, czm, cyp, cym, diag, adj, weighted = refs[2 * REACH :]
    slab = lax.axis_index("slab")

    for f in range(2):
        ext[f, OWN : OWN + ROWS] = mine_ref[f]
        wave[f, OWN : OWN + ROWS, HERE] = mine_ref[f + 2]
    for i, ref in enumerate(near_refs):
        distance, odd = SWAPS[i]
        parity = lax.rem(lax.div(slab, distance), 2)
        side = jnp.where(parity == odd, distance, -distance)
        start = OWN + ROWS * side
        for f in range(2):
            ext[f, pl.ds(start, ROWS)] = ref[f]
            wave[f, pl.ds(start, ROWS), HERE] = ref[f + 2]

    zpos = iota((NZ, NY), 0)
    ypos = iota((NZ, NY), 1)
    z_last, z_first, y_last = zpos == NZ - 1, zpos == 0, ypos == NY - 1
    y_end = 0.5 * (y_last | (ypos == 0)).astype(jnp.float32)
    pad = jnp.zeros((8, NY), jnp.float32)
    for r in range(EXT):
        for n in range(STEPS + 2):
            wave[n, r, 0:8] = pad
            wave[n, r, NZ + 8 : DEEP] = pad
    for r in range(BAND):
        for n in range(3):
            weighted[n, r, 0:8] = pad
            weighted[n, r, NZ + 8 : DEEP] = pad
    for r in range(EXT):
        b = ext[1, r]
        if r + 1 < EXT:
            cx[r] = 0.5 * (b + ext[1, r + 1])
        if 0 < r < EXT - 1:
            up = 0.5 * (b + jnp.where(z_last, 0.0, pltpu.roll(b, NZ - 1, 0)))
            down = 0.5 * (b + jnp.where(z_first, 0.0, pltpu.roll(b, 1, 0)))
            right = jnp.where(y_last, 0.0, 0.5 * (b + up_y(b)))
            left = down_y(right)
            czp[r], czm[r], cyp[r], cym[r] = up, down, right, left
            diag[r] = (cx[r - 1] + cx[r]) + (up + down) + (right + left + y_end * b)

    faces = (cx, czp, czm, cyp, cym, diag)
    local_source = source_ref[0, 0] - (slab * ROWS - OWN) * PLANE
    source_row = jnp.clip(lax.shift_right_arithmetic(local_source, PLANE_BITS), 0, EXT - 1)
    at_source = zpos * NY + ypos == local_source - source_row * PLANE

    def step(n, carry):
        pulse = pulses[pl.ds(n, 1)]

        def emit(r, here, total):
            if OWN <= r < OWN + ROWS:
                lap[n, r - OWN] = total
            wave[n + 2, r, HERE] = (here + here) - wave[n, r, HERE] + ext[0, r] * total

        operate(faces, wave, (n + 1,), 0, 1, EXT - 1, emit)
        wave[n + 2, source_row, HERE] = wave[n + 2, source_row, HERE] + jnp.where(at_source, pulse, 0.0)
        return carry

    lax.fori_loop(0, STEPS, step, 0)

    grad_q = [None] * ROWS
    px = [None] * (ROWS + 1)
    pz = [None] * ROWS
    py = [None] * ROWS
    both = [None] * ROWS

    def add(total, term):
        return term if total is None else total + term

    for k in range(STEPS, 0, -1):
        slot, after, older = k % 3, (k + 1) % 3, (k + 2) % 3

        def residual(r, k=k):
            return count[r - LO] * wave[k + 1, r, HERE] - traces[k - 1, r - LO]

        def store(r, value, slot=slot):
            adj[slot, r - LO] = value
            weighted[slot, r - LO, HERE] = ext[0, r] * value

        if k == STEPS:
            for r in range(OWN - k, OWN + ROWS + k):
                store(r, residual(r))
        else:

            def emit_adj(r, here, total, k=k, after=after, older=older, residual=residual, store=store):
                value = residual(r) + 2.0 * adj[after, r - LO] + total
                if k < STEPS - 1:
                    value = value - adj[older, r - LO]
                store(r, value)

            operate(faces, weighted, (after,), LO, OWN - k, OWN + ROWS + k, emit_adj)

        for a in range(ROWS + 1):
            r = OWN + a
            u, w = wave[k, r, HERE], weighted[slot, r - LO, HERE]
            du = u - wave[k, r - 1, HERE]
            dw = w - weighted[slot, r - 1 - LO, HERE]
            px[a] = add(px[a], du * dw)
            if a < ROWS:
                grad_q[a] = add(grad_q[a], adj[slot, r - LO] * lap[k - 1, a])
                both[a] = add(both[a], u * w)
                pz[a] = add(pz[a], (wave[k, r, UP] - u) * (weighted[slot, r - LO, UP] - w))
                py[a] = add(py[a], (up_y(u) - u) * (up_y(w) - w))

    for a in range(ROWS):
        z_up = pz[a]
        z_down = jnp.where(z_first, both[a], pltpu.roll(pz[a], 1, 0))
        y_up = jnp.where(y_last, both[a], py[a])
        y_down = jnp.where(ypos == 0, both[a], down_y(py[a]))
        grad_b = -0.5 * (((px[a] + px[a + 1]) + (z_up + z_down)) + (y_up + y_down))
        out_ref[a] = grad_q[a]
        out_ref[ROWS + a] = grad_b


def vmem(shape):
    return pltpu.VMEM(shape, jnp.float32)


def swap_pairs(distance, odd):
    pairs = []
    for i in range(SLABS):
        up = (i // distance) % 2 == odd
        j = i + distance if up else i - distance
        if 0 <= j < SLABS:
            pairs.append((i, j))
    return pairs


def local(
    courant,
    buoyancy,
    wave_before,
    wave_now,
    wavelet,
    source_cell,
    observed,
    receiver_slab,
    receiver_cell,
):
    rec = receiver_cell.shape[1]
    mine = jnp.stack([courant, buoyancy, wave_before[0], wave_now[0]])
    near = [lax.ppermute(mine, "slab", swap_pairs(distance, odd)) for distance, odd in SWAPS]
    send = pl.pallas_call(
        route_kernel,
        out_shape=jax.ShapeDtypeStruct((SLABS, 8, 128), jnp.float32),
        name="route",
    )(receiver_slab.reshape(1, rec), receiver_cell, observed.transpose(1, 0, 2))
    got = lax.all_to_all(send, "slab", 0, 0, tiled=True)
    smem = pl.BlockSpec(memory_space=pltpu.SMEM)
    whole = pl.BlockSpec(memory_space=pltpu.VMEM)
    count, traces, pulses = pl.pallas_call(
        scatter_kernel,
        out_shape=(
            jax.ShapeDtypeStruct((BAND, NZ, NY), jnp.float32),
            jax.ShapeDtypeStruct((STEPS, BAND, NZ, NY), jnp.float32),
            jax.ShapeDtypeStruct((8, NY), jnp.float32),
        ),
        in_specs=[smem, whole],
        out_specs=(whole, whole, whole),
        compiler_params=pltpu.CompilerParams(vmem_limit_bytes=24 * 2**20),
        name="scatter",
    )(wavelet, got)
    grads = pl.pallas_call(
        window_kernel,
        out_shape=jax.ShapeDtypeStruct((2 * ROWS, NZ, NY), jnp.float32),
        in_specs=[smem] + [whole] * (2 * REACH + 4),
        out_specs=whole,
        scratch_shapes=[
            vmem((STEPS, ROWS, NZ, NY)),
            vmem((2, EXT, NZ, NY)),
            vmem((STEPS + 2, EXT, DEEP, NY)),
            vmem((EXT, NZ, NY)),
            vmem((EXT, NZ, NY)),
            vmem((EXT, NZ, NY)),
            vmem((EXT, NZ, NY)),
            vmem((EXT, NZ, NY)),
            vmem((EXT, NZ, NY)),
            vmem((3, BAND, NZ, NY)),
            vmem((3, BAND, DEEP, NY)),
        ],
        compiler_params=pltpu.CompilerParams(vmem_limit_bytes=24 * 2**20),
        name="window",
    )(source_cell, mine, *near, count, traces, pulses)
    terms = lax.all_to_all(grads.reshape(SHOTS, 8, NY), "shot", 0, 0, tiled=True)
    total = jnp.broadcast_to(jnp.sum(terms, axis=0), (SHOTS, 8, NY))
    full = lax.all_to_all(total, "shot", 0, 0, tiled=True).reshape(2, ROWS, NZ, NY)
    return full[0], full[1]


def solution(mesh):
    in_specs = (
        P("slab", None, None),
        P("slab", None, None),
        P("shot", "slab", None, None),
        P("shot", "slab", None, None),
        P("shot", None),
        P("shot", None),
        P("shot", None, "slab"),
        P("shot", "slab", None),
        P("shot", "slab"),
    )
    out_specs = (P("slab", None, None), P("slab", None, None))
    return jax.shard_map(local, mesh=mesh, in_specs=in_specs, out_specs=out_specs, check_vma=False)
```

```python
import jax
import jax.numpy as jnp
from jax import lax
from jax.experimental import pallas as pl
from jax.experimental.pallas import tpu as pltpu
from jax.sharding import PartitionSpec as P

STEPS = 6
NZ = 32
NY = 128
ROWS = 4
PLANE = NZ * NY
PLANE_BITS = 12
SLABS = 32
SHOTS = 32
CAP = 32
REACH = 3
EXT = ROWS * (2 * REACH + 1)
OWN = ROWS * REACH
LO = 4
BAND = 20
SHIFTS = (1, -1, 2, -2, 3, -3)

NT = (((1,), (1,)), ((), ()))


def split_bf16(x, pieces):
    out = []
    for _ in range(pieces):
        part = x.astype(jnp.bfloat16)
        out.append(part)
        x = x - part.astype(jnp.float32)
    return out


def iota(shape, axis):
    return lax.broadcasted_iota(jnp.int32, shape, axis)


def mxu(a, b, dims):
    return lax.dot_general(a, b, dims, preferred_element_type=jnp.float32)


def route_kernel(slab_ref, cell_ref, obs_ref, out_ref):
    rec = slab_ref.shape[1]
    slab = slab_ref[...]
    hot = (iota((SLABS, rec), 0) == slab).astype(jnp.float32)
    hot16 = hot.astype(jnp.bfloat16)
    tri = (iota((rec, rec), 0) < iota((rec, rec), 1)).astype(jnp.float32).astype(jnp.bfloat16)
    earlier = mxu(hot16, tri, (((1,), (0,)), ((), ())))
    rank = jnp.sum(earlier * hot, axis=0, keepdims=True).astype(jnp.int32)
    at_slot = iota((CAP, rec), 0) == rank
    cells = (cell_ref[...] + 1).astype(jnp.float32)
    values = [obs_ref[n] for n in range(STEPS)] + [cells]
    total = None
    splits = [split_bf16(v, 3) for v in values]
    for p in range(3):
        rows = [jnp.where(at_slot, s[p].astype(jnp.float32), 0.0) for s in splits]
        rows.append(jnp.zeros((CAP, rec), jnp.float32))
        block = jnp.concatenate(rows, axis=0).astype(jnp.bfloat16)
        term = mxu(hot16, block, NT)
        total = term if total is None else total + term
    row = iota((SLABS, 128), 0)
    lane = iota((SLABS, 128), 1)

    def shifted(tile, shift):
        moved = pltpu.roll(tile, (-shift) % SLABS, 0)
        there = row + shift
        return jnp.where((there >= 0) & (there < SLABS), moved, 0.0)

    tiles = [total[:, 128 * t : 128 * t + 128] for t in range(2)]
    by_shift = {s: [shifted(t, s) if s else t for t in tiles] for s in (-2, -1, 0, 1, 2)}

    def piece(shift, value, group):
        tile = by_shift[shift][value // 4]
        return pltpu.roll(tile, (CAP * (group - value % 4)) % 128, 1) if (group - value % 4) % 4 else tile

    for v in range(8):
        if v < 7:
            near = jnp.where(lane < CAP, piece(-1, v, 0), jnp.where(lane < 2 * CAP, piece(0, v, 1), piece(1, v, 2)))
        else:
            near = jnp.zeros((SLABS, 128), jnp.float32)
        if v < 3:
            far = piece(-2, v + 4, 3)
        elif v < 6:
            far = piece(2, v + 1, 3)
        else:
            far = jnp.zeros((SLABS, 128), jnp.float32)
        out_ref[:, v, :] = jnp.where(lane < 3 * CAP, near, far)


def scatter_dense(cell_row, value_rows, halves):
    count = cell_row.shape[1]
    cell = cell_row.astype(jnp.int32) - 1
    half = lax.shift_right_arithmetic(cell, 13)
    lane_of = cell & 127
    if halves is None:
        spot, width = half * 128 + lane_of, 256
    else:
        spot, width = jnp.where(half == halves, lane_of, -1), 128
    right = (iota((width, count), 0) == spot).astype(jnp.float32).astype(jnp.bfloat16)
    left_hot = iota((64, count), 0) == (lax.shift_right_arithmetic(cell, 7) & 63)
    zero = jnp.zeros((64, count), jnp.float32)
    splits = [split_bf16(v, 2) for v in value_rows]
    blocks = [jnp.where(left_hot, 1.0, zero).astype(jnp.bfloat16)]
    lows = []
    for s in splits:
        blocks.append(jnp.where(left_hot, s[0].astype(jnp.float32), zero).astype(jnp.bfloat16))
        lows.append(jnp.where(left_hot, s[1].astype(jnp.float32), zero).astype(jnp.bfloat16))
    main = mxu(jnp.concatenate(blocks, axis=0), right, NT)
    rest = mxu(jnp.concatenate(lows, axis=0), right, NT)
    out = [main[0:64]]
    for i in range(len(splits)):
        out.append(main[64 * (i + 1) : 64 * (i + 2)] + rest[64 * i : 64 * (i + 1)])
    return out


def scatter_kernel(wavelet_ref, got_ref, count, traces, pulses):
    for n in range(8):
        pulses[n : n + 1] = jnp.full((1, NY), wavelet_ref[0, n] if n < STEPS else 0.0)
    lane8 = iota((8, 128), 1)
    blocks = [[], [], [], []]
    for j in range(SLABS // 4):
        quad = [got_ref[4 * j + i] for i in range(4)]
        for q in range(4):
            merged = None
            for i in range(4):
                turn = (CAP * (i - q)) % 128
                moved = pltpu.roll(quad[i], turn, 1) if turn else quad[i]
                merged = moved if merged is None else jnp.where(lane8 >= CAP * i, moved, merged)
            blocks[q].append(merged)
    lists = [jnp.concatenate(b, axis=1) for b in blocks]
    for q in range(3):
        rows = lists[q]
        parts = scatter_dense(rows[6:7], [rows[n : n + 1] for n in range(STEPS)], None)
        base = OWN + ROWS * (q - 1) - LO
        for i, part in enumerate(parts):
            for a in range(ROWS):
                value = part[NZ * (a % 2) : NZ * (a % 2) + NZ, 128 * (a // 2) : 128 * (a // 2) + 128]
                if i == 0:
                    count[base + a] = value
                else:
                    traces[i - 1, base + a] = value
    for side in range(2):
        rows = lists[3][3 * side : 3 * side + 3]
        parts = scatter_dense(rows[2:3], [rows[0:1], rows[1:2]], 1 - side)
        base = (OWN - 2 * ROWS + 2 if side == 0 else OWN + 2 * ROWS) - LO
        for i, part in enumerate(parts):
            for a in range(2):
                value = part[NZ * a : NZ * a + NZ]
                if i == 0:
                    count[base + a] = value
                else:
                    traces[STEPS - 3 + i, base + a] = value


def up_y(x):
    return pltpu.roll(x, NY - 1, 1)


def down_y(x):
    return pltpu.roll(x, 1, 1)


DEEP = NZ + 16
HERE = pl.ds(8, NZ)
UP = pl.ds(9, NZ)
DOWN = pl.ds(7, NZ)


def operate(faces, field, rows, base, lo, hi, emit):
    cx, czp, czm, cyp, cym, diag = faces
    before, here = field[(*rows, lo - 1 - base, HERE)], field[(*rows, lo - base, HERE)]
    for r in range(lo, hi):
        after = field[(*rows, r + 1 - base, HERE)]
        total = cx[r] * after + cx[r - 1] * before
        total += czp[r] * field[(*rows, r - base, UP)] + czm[r] * field[(*rows, r - base, DOWN)]
        total += cyp[r] * up_y(here) + cym[r] * down_y(here)
        emit(r, here, total - diag[r] * here)
        before, here = here, after


def window_kernel(source_ref, mine_ref, *refs):
    near_refs = refs[: 2 * REACH]
    count, traces, pulses, out_ref, lap, ext, wave, cx, czp, czm, cyp, cym, diag, adj, weighted = refs[2 * REACH :]
    slab = lax.axis_index("slab")

    for f in range(2):
        ext[f, OWN : OWN + ROWS] = mine_ref[f]
        wave[f, OWN : OWN + ROWS, HERE] = mine_ref[f + 2]
    for i, ref in enumerate(near_refs):
        start = OWN - ROWS * SHIFTS[i]
        for f in range(2):
            ext[f, start : start + ROWS] = ref[f]
            wave[f, start : start + ROWS, HERE] = ref[f + 2]

    zpos = iota((NZ, NY), 0)
    ypos = iota((NZ, NY), 1)
    z_last, z_first, y_last = zpos == NZ - 1, zpos == 0, ypos == NY - 1
    y_end = 0.5 * (y_last | (ypos == 0)).astype(jnp.float32)
    pad = jnp.zeros((8, NY), jnp.float32)
    for r in range(EXT):
        for n in range(STEPS + 2):
            wave[n, r, 0:8] = pad
            wave[n, r, NZ + 8 : DEEP] = pad
    for r in range(BAND):
        for n in range(3):
            weighted[n, r, 0:8] = pad
            weighted[n, r, NZ + 8 : DEEP] = pad
    for r in range(EXT):
        b = ext[1, r]
        if r + 1 < EXT:
            cx[r] = 0.5 * (b + ext[1, r + 1])
        if 0 < r < EXT - 1:
            up = 0.5 * (b + jnp.where(z_last, 0.0, pltpu.roll(b, NZ - 1, 0)))
            down = 0.5 * (b + jnp.where(z_first, 0.0, pltpu.roll(b, 1, 0)))
            right = jnp.where(y_last, 0.0, 0.5 * (b + up_y(b)))
            left = down_y(right)
            czp[r], czm[r], cyp[r], cym[r] = up, down, right, left
            diag[r] = (cx[r - 1] + cx[r]) + (up + down) + (right + left + y_end * b)

    faces = (cx, czp, czm, cyp, cym, diag)
    local_source = source_ref[0, 0] - (slab * ROWS - OWN) * PLANE
    source_row = jnp.clip(lax.shift_right_arithmetic(local_source, PLANE_BITS), 0, EXT - 1)
    at_source = zpos * NY + ypos == local_source - source_row * PLANE

    def step(n, carry):
        pulse = pulses[pl.ds(n, 1)]

        def emit(r, here, total):
            if OWN <= r < OWN + ROWS:
                lap[n, r - OWN] = total
            wave[n + 2, r, HERE] = (here + here) - wave[n, r, HERE] + ext[0, r] * total

        operate(faces, wave, (n + 1,), 0, 1, EXT - 1, emit)
        wave[n + 2, source_row, HERE] = wave[n + 2, source_row, HERE] + jnp.where(at_source, pulse, 0.0)
        return carry

    lax.fori_loop(0, STEPS, step, 0)

    grad_q = [None] * ROWS
    px = [None] * (ROWS + 1)
    pz = [None] * ROWS
    py = [None] * ROWS
    both = [None] * ROWS

    def add(total, term):
        return term if total is None else total + term

    for k in range(STEPS, 0, -1):
        slot, after, older = k % 3, (k + 1) % 3, (k + 2) % 3

        def residual(r, k=k):
            return count[r - LO] * wave[k + 1, r, HERE] - traces[k - 1, r - LO]

        def store(r, value, slot=slot):
            adj[slot, r - LO] = value
            weighted[slot, r - LO, HERE] = ext[0, r] * value

        if k == STEPS:
            for r in range(OWN - k, OWN + ROWS + k):
                store(r, residual(r))
        else:

            def emit_adj(r, here, total, k=k, after=after, older=older, residual=residual, store=store):
                value = residual(r) + 2.0 * adj[after, r - LO] + total
                if k < STEPS - 1:
                    value = value - adj[older, r - LO]
                store(r, value)

            operate(faces, weighted, (after,), LO, OWN - k, OWN + ROWS + k, emit_adj)

        for a in range(ROWS + 1):
            r = OWN + a
            u, w = wave[k, r, HERE], weighted[slot, r - LO, HERE]
            du = u - wave[k, r - 1, HERE]
            dw = w - weighted[slot, r - 1 - LO, HERE]
            px[a] = add(px[a], du * dw)
            if a < ROWS:
                grad_q[a] = add(grad_q[a], adj[slot, r - LO] * lap[k - 1, a])
                both[a] = add(both[a], u * w)
                pz[a] = add(pz[a], (wave[k, r, UP] - u) * (weighted[slot, r - LO, UP] - w))
                py[a] = add(py[a], (up_y(u) - u) * (up_y(w) - w))

    for a in range(ROWS):
        z_up = pz[a]
        z_down = jnp.where(z_first, both[a], pltpu.roll(pz[a], 1, 0))
        y_up = jnp.where(y_last, both[a], py[a])
        y_down = jnp.where(ypos == 0, both[a], down_y(py[a]))
        grad_b = -0.5 * (((px[a] + px[a + 1]) + (z_up + z_down)) + (y_up + y_down))
        out_ref[a] = grad_q[a]
        out_ref[ROWS + a] = grad_b


def vmem(shape):
    return pltpu.VMEM(shape, jnp.float32)


def shift_pairs(shift):
    return [(i, i + shift) for i in range(SLABS) if 0 <= i + shift < SLABS]


def local(
    courant,
    buoyancy,
    wave_before,
    wave_now,
    wavelet,
    source_cell,
    observed,
    receiver_slab,
    receiver_cell,
):
    rec = receiver_cell.shape[1]
    mine = jnp.stack([courant, buoyancy, wave_before[0], wave_now[0]])
    near = [lax.ppermute(mine, "slab", shift_pairs(shift)) for shift in SHIFTS]
    send = pl.pallas_call(
        route_kernel,
        out_shape=jax.ShapeDtypeStruct((SLABS, 8, 128), jnp.float32),
        name="route",
    )(receiver_slab.reshape(1, rec), receiver_cell, observed.transpose(1, 0, 2))
    got = lax.all_to_all(send, "slab", 0, 0, tiled=True)
    smem = pl.BlockSpec(memory_space=pltpu.SMEM)
    whole = pl.BlockSpec(memory_space=pltpu.VMEM)
    count, traces, pulses = pl.pallas_call(
        scatter_kernel,
        out_shape=(
            jax.ShapeDtypeStruct((BAND, NZ, NY), jnp.float32),
            jax.ShapeDtypeStruct((STEPS, BAND, NZ, NY), jnp.float32),
            jax.ShapeDtypeStruct((8, NY), jnp.float32),
        ),
        in_specs=[smem, whole],
        out_specs=(whole, whole, whole),
        compiler_params=pltpu.CompilerParams(vmem_limit_bytes=24 * 2**20),
        name="scatter",
    )(wavelet, got)
    grads = pl.pallas_call(
        window_kernel,
        out_shape=jax.ShapeDtypeStruct((2 * ROWS, NZ, NY), jnp.float32),
        in_specs=[smem] + [whole] * (2 * REACH + 4),
        out_specs=whole,
        scratch_shapes=[
            vmem((STEPS, ROWS, NZ, NY)),
            vmem((2, EXT, NZ, NY)),
            vmem((STEPS + 2, EXT, DEEP, NY)),
            vmem((EXT, NZ, NY)),
            vmem((EXT, NZ, NY)),
            vmem((EXT, NZ, NY)),
            vmem((EXT, NZ, NY)),
            vmem((EXT, NZ, NY)),
            vmem((EXT, NZ, NY)),
            vmem((3, BAND, NZ, NY)),
            vmem((3, BAND, DEEP, NY)),
        ],
        compiler_params=pltpu.CompilerParams(vmem_limit_bytes=24 * 2**20),
        name="window",
    )(source_cell, mine, *near, count, traces, pulses)
    terms = lax.all_to_all(grads.reshape(SHOTS, 8, NY), "shot", 0, 0, tiled=True)
    total = jnp.broadcast_to(jnp.sum(terms, axis=0), (SHOTS, 8, NY))
    full = lax.all_to_all(total, "shot", 0, 0, tiled=True).reshape(2, ROWS, NZ, NY)
    return full[0], full[1]


def solution(mesh):
    in_specs = (
        P("slab", None, None),
        P("slab", None, None),
        P("shot", "slab", None, None),
        P("shot", "slab", None, None),
        P("shot", None),
        P("shot", None),
        P("shot", None, "slab"),
        P("shot", "slab", None),
        P("shot", "slab"),
    )
    out_specs = (P("slab", None, None), P("slab", None, None))
    return jax.shard_map(local, mesh=mesh, in_specs=in_specs, out_specs=out_specs, check_vma=False)
```

```python
import jax
import jax.numpy as jnp
from jax import lax
from jax.experimental import pallas as pl
from jax.experimental.pallas import tpu as pltpu
from jax.sharding import PartitionSpec as P

STEPS = 6
NZ = 32
NY = 128
ROWS = 4
PLANE = NZ * NY
PLANE_BITS = 12
SLABS = 32
SHOTS = 32
CAP = 32
REACH = 3
EXT = ROWS * (2 * REACH + 1)
OWN = ROWS * REACH
LO = 4
BAND = 20
SHIFTS = (3, -3, 1, -1, 2, -2)

NT = (((1,), (1,)), ((), ()))


def split_bf16(x, pieces):
    out = []
    for _ in range(pieces):
        part = x.astype(jnp.bfloat16)
        out.append(part)
        x = x - part.astype(jnp.float32)
    return out


def iota(shape, axis):
    return lax.broadcasted_iota(jnp.int32, shape, axis)


def mxu(a, b, dims):
    return lax.dot_general(a, b, dims, preferred_element_type=jnp.float32)


def route_kernel(slab_ref, cell_ref, obs_ref, out_ref):
    rec = slab_ref.shape[1]
    slab = slab_ref[...]
    hot = (iota((SLABS, rec), 0) == slab).astype(jnp.float32)
    hot16 = hot.astype(jnp.bfloat16)
    tri = (iota((rec, rec), 0) < iota((rec, rec), 1)).astype(jnp.float32).astype(jnp.bfloat16)
    earlier = mxu(hot16, tri, (((1,), (0,)), ((), ())))
    rank = jnp.sum(earlier * hot, axis=0, keepdims=True).astype(jnp.int32)
    at_slot = iota((CAP, rec), 0) == rank
    cells = (cell_ref[...] + 1).astype(jnp.float32)
    values = [obs_ref[n] for n in range(STEPS)] + [cells]
    total = None
    splits = [split_bf16(v, 2) for v in values]
    for p in range(2):
        rows = [jnp.where(at_slot, s[p].astype(jnp.float32), 0.0) for s in splits]
        rows.append(jnp.zeros((CAP, rec), jnp.float32))
        block = jnp.concatenate(rows, axis=0).astype(jnp.bfloat16)
        term = mxu(hot16, block, NT)
        total = term if total is None else total + term
    row = iota((SLABS, 128), 0)
    lane = iota((SLABS, 128), 1)

    def shifted(tile, shift):
        moved = pltpu.roll(tile, (-shift) % SLABS, 0)
        there = row + shift
        return jnp.where((there >= 0) & (there < SLABS), moved, 0.0)

    tiles = [total[:, 128 * t : 128 * t + 128] for t in range(2)]
    by_shift = {s: [shifted(t, s) if s else t for t in tiles] for s in (-2, -1, 0, 1, 2)}

    def piece(shift, value, group):
        tile = by_shift[shift][value // 4]
        return pltpu.roll(tile, (CAP * (group - value % 4)) % 128, 1) if (group - value % 4) % 4 else tile

    for v in range(8):
        if v < 7:
            near = jnp.where(lane < CAP, piece(-1, v, 0), jnp.where(lane < 2 * CAP, piece(0, v, 1), piece(1, v, 2)))
        else:
            near = jnp.zeros((SLABS, 128), jnp.float32)
        if v < 3:
            far = piece(-2, v + 4, 3)
        elif v < 6:
            far = piece(2, v + 1, 3)
        else:
            far = jnp.zeros((SLABS, 128), jnp.float32)
        out_ref[:, v, :] = jnp.where(lane < 3 * CAP, near, far)


def scatter_dense(cell_row, value_rows, halves):
    count = cell_row.shape[1]
    cell = cell_row.astype(jnp.int32) - 1
    half = lax.shift_right_arithmetic(cell, 13)
    lane_of = cell & 127
    if halves is None:
        spot, width = half * 128 + lane_of, 256
    else:
        spot, width = jnp.where(half == halves, lane_of, -1), 128
    right = (iota((width, count), 0) == spot).astype(jnp.float32).astype(jnp.bfloat16)
    left_hot = iota((64, count), 0) == (lax.shift_right_arithmetic(cell, 7) & 63)
    zero = jnp.zeros((64, count), jnp.float32)
    splits = [split_bf16(v, 2) for v in value_rows]
    blocks = [jnp.where(left_hot, 1.0, zero).astype(jnp.bfloat16)]
    lows = []
    for s in splits:
        blocks.append(jnp.where(left_hot, s[0].astype(jnp.float32), zero).astype(jnp.bfloat16))
        lows.append(jnp.where(left_hot, s[1].astype(jnp.float32), zero).astype(jnp.bfloat16))
    main = mxu(jnp.concatenate(blocks, axis=0), right, NT)
    rest = mxu(jnp.concatenate(lows, axis=0), right, NT)
    out = [main[0:64]]
    for i in range(len(splits)):
        out.append(main[64 * (i + 1) : 64 * (i + 2)] + rest[64 * i : 64 * (i + 1)])
    return out


def scatter_kernel(wavelet_ref, got_ref, count, traces, pulses):
    for n in range(8):
        pulses[n : n + 1] = jnp.full((1, NY), wavelet_ref[0, n] if n < STEPS else 0.0)
    lane8 = iota((8, 128), 1)
    blocks = [[], [], [], []]
    for j in range(SLABS // 4):
        quad = [got_ref[4 * j + i] for i in range(4)]
        for q in range(4):
            merged = None
            for i in range(4):
                turn = (CAP * (i - q)) % 128
                moved = pltpu.roll(quad[i], turn, 1) if turn else quad[i]
                merged = moved if merged is None else jnp.where(lane8 >= CAP * i, moved, merged)
            blocks[q].append(merged)
    lists = [jnp.concatenate(b, axis=1) for b in blocks]
    for q in range(3):
        rows = lists[q]
        parts = scatter_dense(rows[6:7], [rows[n : n + 1] for n in range(STEPS)], None)
        base = OWN + ROWS * (q - 1) - LO
        for i, part in enumerate(parts):
            for a in range(ROWS):
                value = part[NZ * (a % 2) : NZ * (a % 2) + NZ, 128 * (a // 2) : 128 * (a // 2) + 128]
                if i == 0:
                    count[base + a] = value
                else:
                    traces[i - 1, base + a] = value
    for side in range(2):
        rows = lists[3][3 * side : 3 * side + 3]
        parts = scatter_dense(rows[2:3], [rows[0:1], rows[1:2]], 1 - side)
        base = (OWN - 2 * ROWS + 2 if side == 0 else OWN + 2 * ROWS) - LO
        for i, part in enumerate(parts):
            for a in range(2):
                value = part[NZ * a : NZ * a + NZ]
                if i == 0:
                    count[base + a] = value
                else:
                    traces[STEPS - 3 + i, base + a] = value


def up_y(x):
    return pltpu.roll(x, NY - 1, 1)


def down_y(x):
    return pltpu.roll(x, 1, 1)


DEEP = NZ + 16
HERE = pl.ds(8, NZ)
UP = pl.ds(9, NZ)
DOWN = pl.ds(7, NZ)


def operate(faces, field, rows, base, lo, hi, emit):
    cx, czp, czm, cyp, cym, diag = faces
    before, here = field[(*rows, lo - 1 - base, HERE)], field[(*rows, lo - base, HERE)]
    for r in range(lo, hi):
        after = field[(*rows, r + 1 - base, HERE)]
        total = cx[r] * after + cx[r - 1] * before
        total += czp[r] * field[(*rows, r - base, UP)] + czm[r] * field[(*rows, r - base, DOWN)]
        total += cyp[r] * up_y(here) + cym[r] * down_y(here)
        emit(r, here, total - diag[r] * here)
        before, here = here, after


def window_kernel(source_ref, mine_ref, *refs):
    near_refs = refs[: 2 * REACH]
    count, traces, pulses, out_ref, lap, ext, wave, cx, czp, czm, cyp, cym, diag, adj, weighted = refs[2 * REACH :]
    slab = lax.axis_index("slab")

    for f in range(2):
        ext[f, OWN : OWN + ROWS] = mine_ref[f]
        wave[f, OWN : OWN + ROWS, HERE] = mine_ref[f + 2]
    for i, ref in enumerate(near_refs):
        start = OWN - ROWS * SHIFTS[i]
        for f in range(2):
            ext[f, start : start + ROWS] = ref[f]
            wave[f, start : start + ROWS, HERE] = ref[f + 2]

    zpos = iota((NZ, NY), 0)
    ypos = iota((NZ, NY), 1)
    z_last, z_first, y_last = zpos == NZ - 1, zpos == 0, ypos == NY - 1
    y_end = 0.5 * (y_last | (ypos == 0)).astype(jnp.float32)
    pad = jnp.zeros((8, NY), jnp.float32)
    for r in range(EXT):
        for n in range(STEPS + 2):
            wave[n, r, 0:8] = pad
            wave[n, r, NZ + 8 : DEEP] = pad
    for r in range(BAND):
        for n in range(3):
            weighted[n, r, 0:8] = pad
            weighted[n, r, NZ + 8 : DEEP] = pad
    for r in range(EXT):
        b = ext[1, r]
        if r + 1 < EXT:
            cx[r] = 0.5 * (b + ext[1, r + 1])
        if 0 < r < EXT - 1:
            up = 0.5 * (b + jnp.where(z_last, 0.0, pltpu.roll(b, NZ - 1, 0)))
            down = 0.5 * (b + jnp.where(z_first, 0.0, pltpu.roll(b, 1, 0)))
            right = jnp.where(y_last, 0.0, 0.5 * (b + up_y(b)))
            left = down_y(right)
            czp[r], czm[r], cyp[r], cym[r] = up, down, right, left
            diag[r] = (cx[r - 1] + cx[r]) + (up + down) + (right + left + y_end * b)

    faces = (cx, czp, czm, cyp, cym, diag)
    local_source = source_ref[0, 0] - (slab * ROWS - OWN) * PLANE
    source_row = jnp.clip(lax.shift_right_arithmetic(local_source, PLANE_BITS), 0, EXT - 1)
    at_source = zpos * NY + ypos == local_source - source_row * PLANE

    def step(n, carry):
        pulse = pulses[pl.ds(n, 1)]

        def emit(r, here, total):
            if OWN <= r < OWN + ROWS:
                lap[n, r - OWN] = total
            wave[n + 2, r, HERE] = (here + here) - wave[n, r, HERE] + ext[0, r] * total

        operate(faces, wave, (n + 1,), 0, 1, EXT - 1, emit)
        wave[n + 2, source_row, HERE] = wave[n + 2, source_row, HERE] + jnp.where(at_source, pulse, 0.0)
        return carry

    lax.fori_loop(0, STEPS, step, 0)

    grad_q = [None] * ROWS
    px = [None] * (ROWS + 1)
    pz = [None] * ROWS
    py = [None] * ROWS
    both = [None] * ROWS

    def add(total, term):
        return term if total is None else total + term

    for k in range(STEPS, 0, -1):
        slot, after, older = k % 3, (k + 1) % 3, (k + 2) % 3

        def residual(r, k=k):
            return count[r - LO] * wave[k + 1, r, HERE] - traces[k - 1, r - LO]

        def store(r, value, slot=slot):
            adj[slot, r - LO] = value
            weighted[slot, r - LO, HERE] = ext[0, r] * value

        if k == STEPS:
            for r in range(OWN - k, OWN + ROWS + k):
                store(r, residual(r))
        else:

            def emit_adj(r, here, total, k=k, after=after, older=older, residual=residual, store=store):
                value = residual(r) + 2.0 * adj[after, r - LO] + total
                if k < STEPS - 1:
                    value = value - adj[older, r - LO]
                store(r, value)

            operate(faces, weighted, (after,), LO, OWN - k, OWN + ROWS + k, emit_adj)

        for a in range(ROWS + 1):
            r = OWN + a
            u, w = wave[k, r, HERE], weighted[slot, r - LO, HERE]
            du = u - wave[k, r - 1, HERE]
            dw = w - weighted[slot, r - 1 - LO, HERE]
            px[a] = add(px[a], du * dw)
            if a < ROWS:
                grad_q[a] = add(grad_q[a], adj[slot, r - LO] * lap[k - 1, a])
                both[a] = add(both[a], u * w)
                pz[a] = add(pz[a], (wave[k, r, UP] - u) * (weighted[slot, r - LO, UP] - w))
                py[a] = add(py[a], (up_y(u) - u) * (up_y(w) - w))

    for a in range(ROWS):
        z_up = pz[a]
        z_down = jnp.where(z_first, both[a], pltpu.roll(pz[a], 1, 0))
        y_up = jnp.where(y_last, both[a], py[a])
        y_down = jnp.where(ypos == 0, both[a], down_y(py[a]))
        grad_b = -0.5 * (((px[a] + px[a + 1]) + (z_up + z_down)) + (y_up + y_down))
        out_ref[a] = grad_q[a]
        out_ref[ROWS + a] = grad_b


def vmem(shape):
    return pltpu.VMEM(shape, jnp.float32)


def shift_pairs(shift):
    return [(i, i + shift) for i in range(SLABS) if 0 <= i + shift < SLABS]


def local(
    courant,
    buoyancy,
    wave_before,
    wave_now,
    wavelet,
    source_cell,
    observed,
    receiver_slab,
    receiver_cell,
):
    rec = receiver_cell.shape[1]
    mine = jnp.stack([courant, buoyancy, wave_before[0], wave_now[0]])
    near = [lax.ppermute(mine, "slab", shift_pairs(shift)) for shift in SHIFTS]
    send = pl.pallas_call(
        route_kernel,
        out_shape=jax.ShapeDtypeStruct((SLABS, 8, 128), jnp.float32),
        name="route",
    )(receiver_slab.reshape(1, rec), receiver_cell, observed.transpose(1, 0, 2))
    got = lax.all_to_all(send, "slab", 0, 0, tiled=True)
    smem = pl.BlockSpec(memory_space=pltpu.SMEM)
    whole = pl.BlockSpec(memory_space=pltpu.VMEM)
    count, traces, pulses = pl.pallas_call(
        scatter_kernel,
        out_shape=(
            jax.ShapeDtypeStruct((BAND, NZ, NY), jnp.float32),
            jax.ShapeDtypeStruct((STEPS, BAND, NZ, NY), jnp.float32),
            jax.ShapeDtypeStruct((8, NY), jnp.float32),
        ),
        in_specs=[smem, whole],
        out_specs=(whole, whole, whole),
        compiler_params=pltpu.CompilerParams(vmem_limit_bytes=24 * 2**20),
        name="scatter",
    )(wavelet, got)
    grads = pl.pallas_call(
        window_kernel,
        out_shape=jax.ShapeDtypeStruct((2 * ROWS, NZ, NY), jnp.float32),
        in_specs=[smem] + [whole] * (2 * REACH + 4),
        out_specs=whole,
        scratch_shapes=[
            vmem((STEPS, ROWS, NZ, NY)),
            vmem((2, EXT, NZ, NY)),
            vmem((STEPS + 2, EXT, DEEP, NY)),
            vmem((EXT, NZ, NY)),
            vmem((EXT, NZ, NY)),
            vmem((EXT, NZ, NY)),
            vmem((EXT, NZ, NY)),
            vmem((EXT, NZ, NY)),
            vmem((EXT, NZ, NY)),
            vmem((3, BAND, NZ, NY)),
            vmem((3, BAND, DEEP, NY)),
        ],
        compiler_params=pltpu.CompilerParams(vmem_limit_bytes=24 * 2**20),
        name="window",
    )(source_cell, mine, *near, count, traces, pulses)
    terms = lax.all_to_all(grads.reshape(SHOTS, 8, NY), "shot", 0, 0, tiled=True)
    total = jnp.broadcast_to(jnp.sum(terms, axis=0), (SHOTS, 8, NY))
    full = lax.all_to_all(total, "shot", 0, 0, tiled=True).reshape(2, ROWS, NZ, NY)
    return full[0], full[1]


def solution(mesh):
    in_specs = (
        P("slab", None, None),
        P("slab", None, None),
        P("shot", "slab", None, None),
        P("shot", "slab", None, None),
        P("shot", None),
        P("shot", None),
        P("shot", None, "slab"),
        P("shot", "slab", None),
        P("shot", "slab"),
    )
    out_specs = (P("slab", None, None), P("slab", None, None))
    return jax.shard_map(local, mesh=mesh, in_specs=in_specs, out_specs=out_specs, check_vma=False)
```
